128 devices in a mesh: tile: 32 (over y, z, x_lo), therm: 4 (over x_hi, core).
Axes of the slice: x: 4 (x_hi: 2, x_lo: 2; x = x_hi * 2 + x_lo), y: 4, z: 4, core: 2. Of those that a mesh axis runs over, the one named last changes fastest.
Arguments:
- sink_current: float32 [12, 1024, 1024], P('therm', 'tile'), may hold values from 0 to 60, as said below
- metal_category: int32 [12, 1024, 1024], P('therm', 'tile'), may hold values from 0 to 7
- upward_link_flag: int32 [12, 1024, 1024], P('therm', 'tile'), may hold values 0 or 1
- supply_contact_flag: int32 [12, 1024, 1024], P('therm', 'tile'), may hold values 0 or 1
- baseline_admittance: float32 [8], replicated, may hold values from 0.3 to 3
- beginning_warmth: float32 [64, 1024, 1024], P('therm', 'tile'), may hold values from 0.5 to 4
- cell_diffusivity: float32 [64, 1024, 1024], P('therm', 'tile'), may hold values from 0.5 to 2
- dissipation_split: float32 [64, 12], replicated, may hold values from 0.1 to 1
- probe_weighting: float32 [12, 64], replicated, may hold values from 0.005 to 0.05
Outputs:
- voltage_loss: float32 [12, 1024, 1024], P('therm', 'tile')
- final_warmth: float32 [64, 1024, 1024], P('therm', 'tile')
- updated_admittance: float32 [12, 1024, 1024], P('therm', 'tile')
The draws below stay inside these ranges and needn't reach their ends.
Inputs may be any that keep to these rules, and one draw needn't show every extreme that they name: `sink_current`: positive load currents.
All inputs are finite; a program needn't handle non-finite values. No bound on the sum of `upward_link_flag` or of `supply_contact_flag` on one device may be relied on, other than what follows from the above.
Results may differ from the reference program's by a relative error of at most 0.0003.
Values sent between devices are 32-bit elements; how exact they have to be, the bound alone decides.
No kernel may reach another device: no remote copies, remote signals or barrier semaphores. Data moves between devices by JAX's collectives and lax.ppermute only.
A program may use at most 192 MiB of HBM per device.

```python
import math
import jax
import jax.numpy as jnp
from jax import lax

DIE_WIDTH = 1024
L = 12
STRATA_COUNT = 64
NCLASS = 8
ITERS = 3
SWEEPS = 4
DIE_HEIGHT = 1024


def draw_sink_current(key, part):
    key = jax.random.fold_in(key, 1)
    layer_place = jnp.arange(L, dtype=jnp.float32)[:, None, None] / L
    row_place = jnp.arange(DIE_HEIGHT, dtype=jnp.float32)[None, :, None] / DIE_HEIGHT
    currents = jnp.exp(jax.random.uniform(key, (L, DIE_HEIGHT, DIE_WIDTH), jnp.float32, math.log(0.05), math.log(2.0)))
    rising = 1.0 + 2.0 * row_place
    return currents * rising * (1.0 + 2.0 * layer_place)


def with_ends(entries, stream_key, least, top_value):
    longest = entries.shape.index(max(entries.shape))
    spots = []
    for shift in (0, 1):
        where = [jax.random.randint(jax.random.fold_in(stream_key, axis), (), 0, length) for axis, length in enumerate(entries.shape)]
        where[longest] = (where[longest] + shift) % entries.shape[longest]
        spots.append(tuple(where))
    return entries.at[spots[0]].set(least).at[spots[1]].set(top_value)


def block_levels(own_key, shape, pieces, low, high):
    def one(position, blocks):
        draws = jax.random.uniform(jax.random.fold_in(jax.random.fold_in(own_key, 6), position), (blocks,), jnp.float32, low / len(pieces), high / len(pieces))
        return jnp.repeat(jnp.exp(draws), shape[position] // blocks).reshape((-1,) + (1,) * (len(shape) - position - 1))

    gain = one(*pieces[0])
    for cut in pieces[1:]:
        gain = gain * one(*cut)
    return gain


def setup_inputs(seed: int = 0) -> dict:
    streams_of = jax.random.split(jax.random.key(seed), 10)
    sink_current = draw_sink_current(jax.random.fold_in(streams_of[9], 71), 0)
    metal_category = with_ends(jax.random.randint(streams_of[1], (L, DIE_HEIGHT, DIE_WIDTH), 0, NCLASS), jax.random.fold_in(streams_of[1], 1), 0, NCLASS - 1).astype(jnp.int32)
    upward_link_flag = with_ends((jax.random.randint(streams_of[2], (L, DIE_HEIGHT, DIE_WIDTH), 0, 2) < 1).astype(jnp.int32), jax.random.fold_in(streams_of[2], 1), 0, 1)
    supply_contact_flag = with_ends((jax.random.randint(streams_of[3], (L, DIE_HEIGHT, DIE_WIDTH), 0, 8) < 1).astype(jnp.int32), jax.random.fold_in(streams_of[3], 1), 0, 1)
    baseline_admittance = jnp.clip(jnp.exp(jax.random.uniform(streams_of[4], (NCLASS,), jnp.float32, math.log(0.3), math.log(3.0))), 0.3, 3.0)
    beginning_warmth = jnp.clip(0.5 + 3.5 * jax.random.uniform(streams_of[5], (STRATA_COUNT, DIE_HEIGHT, DIE_WIDTH), jnp.float32) ** block_levels(streams_of[5], (STRATA_COUNT, DIE_HEIGHT, DIE_WIDTH), ((0, 4), (1, 32)), -0.2, 0.2), 0.5, 4.0)
    cell_diffusivity = jnp.clip(jnp.exp(math.log(2.0) - 1.3862944 * jax.random.uniform(streams_of[6], (STRATA_COUNT, DIE_HEIGHT, DIE_WIDTH), jnp.float32) ** block_levels(streams_of[6], (STRATA_COUNT, DIE_HEIGHT, DIE_WIDTH), ((0, 4), (1, 32)), -0.2, 0.2)), 0.5, 2.0)
    dissipation_split = jnp.clip(jnp.exp(jax.random.uniform(streams_of[7], (STRATA_COUNT, L), jnp.float32, math.log(0.1), math.log(1.0))), 0.1, 1.0)
    probe_weighting = jnp.clip(jnp.exp(jax.random.uniform(streams_of[8], (L, STRATA_COUNT), jnp.float32, math.log(0.005), math.log(0.05))), 0.005, 0.05)
    return {"sink_current": sink_current, "metal_category": metal_category, "upward_link_flag": upward_link_flag, "supply_contact_flag": supply_contact_flag, "baseline_admittance": baseline_admittance, "beginning_warmth": beginning_warmth, "cell_diffusivity": cell_diffusivity, "dissipation_split": dissipation_split, "probe_weighting": probe_weighting}


shunt_level = 0.05
pad_conductance = 4.0
via_conductance = 2.0
thermal_slope = 0.2
sink_level = 0.1


def harmonic(first, second):
    return first * second / (first + second)


def observed_energy(probe_weighting, field):
    return jnp.einsum("lz,zxy->lxy", probe_weighting, field, precision=lax.Precision.HIGHEST)


def reference(sink_current, metal_category, upward_link_flag, supply_contact_flag, baseline_admittance, beginning_warmth, cell_diffusivity, dissipation_split, probe_weighting):
    power_density = observed_energy(probe_weighting, beginning_warmth)
    lateral = baseline_admittance[metal_category] / (1.0 + thermal_slope * power_density)
    vertical = upward_link_flag.astype(jnp.float32) * via_conductance / (1.0 + thermal_slope * power_density)
    below = jnp.pad(vertical, ((1, 0), (0, 0), (0, 0)))[:-1]
    grounded = shunt_level + supply_contact_flag.astype(jnp.float32) * pad_conductance
    padded = jnp.pad(lateral, ((0, 0), (1, 1), (1, 1)))
    row_edges = harmonic(padded[:, :-1, 1:-1], padded[:, 1:, 1:-1])
    col_edges = harmonic(padded[:, 1:-1, :-1], padded[:, 1:-1, 1:])
    diagonal = grounded + vertical + below + row_edges[:, :-1] + row_edges[:, 1:] + col_edges[..., :-1] + col_edges[..., 1:]

    def operate(field):
        beside_all = jnp.pad(field, 1)
        result = diagonal * field - row_edges[:, :-1] * beside_all[1:-1, :-2, 1:-1] - row_edges[:, 1:] * beside_all[1:-1, 2:, 1:-1]
        result = result - col_edges[..., :-1] * beside_all[1:-1, 1:-1, :-2] - col_edges[..., 1:] * beside_all[1:-1, 1:-1, 2:]
        return result - vertical * beside_all[2:, 1:-1, 1:-1] - below * beside_all[:-2, 1:-1, 1:-1]

    voltage_loss = jnp.zeros_like(sink_current)
    residual = sink_current
    direction = sink_current
    norm_now = jnp.sum(residual * residual)
    for step in range(ITERS):
        image = operate(direction)
        alpha = norm_now / jnp.sum(direction * image)
        voltage_loss = voltage_loss + alpha * direction
        residual = residual - alpha * image
        norm_next = jnp.sum(residual * residual)
        direction = residual + (norm_next / norm_now) * direction
        norm_now = norm_next

    beside_all = jnp.pad(voltage_loss, 1)
    diffs = [
        (row_edges[:, :-1], beside_all[1:-1, :-2, 1:-1]),
        (row_edges[:, 1:], beside_all[1:-1, 2:, 1:-1]),
        (col_edges[..., :-1], beside_all[1:-1, 1:-1, :-2]),
        (col_edges[..., 1:], beside_all[1:-1, 1:-1, 2:]),
        (vertical, beside_all[2:, 1:-1, 1:-1]),
        (below, beside_all[:-2, 1:-1, 1:-1]),
    ]
    edge_power = jnp.zeros_like(voltage_loss)
    for edge, other in diffs:
        edge_power = edge_power + edge * (voltage_loss - other) * (voltage_loss - other)
    power = grounded * voltage_loss * voltage_loss + 0.5 * edge_power

    source = jnp.einsum("zl,lxy->zxy", dissipation_split, power, precision=lax.Precision.HIGHEST)
    kpad = jnp.pad(cell_diffusivity, 1)
    depth_edges = harmonic(kpad[:-1, 1:-1, 1:-1], kpad[1:, 1:-1, 1:-1])
    row_heat = harmonic(kpad[1:-1, :-1, 1:-1], kpad[1:-1, 1:, 1:-1])
    col_heat = harmonic(kpad[1:-1, 1:-1, :-1], kpad[1:-1, 1:-1, 1:])
    overall_total = sink_level + depth_edges[:-1] + depth_edges[1:] + row_heat[:, :-1] + row_heat[:, 1:] + col_heat[..., :-1] + col_heat[..., 1:]
    final_warmth = beginning_warmth
    for sweep in range(SWEEPS):
        warmth_fringe = jnp.pad(final_warmth, 1)
        inward_current_flow = source + depth_edges[:-1] * warmth_fringe[:-2, 1:-1, 1:-1] + depth_edges[1:] * warmth_fringe[2:, 1:-1, 1:-1]
        inward_current_flow = inward_current_flow + row_heat[:, :-1] * warmth_fringe[1:-1, :-2, 1:-1] + row_heat[:, 1:] * warmth_fringe[1:-1, 2:, 1:-1]
        inward_current_flow = inward_current_flow + col_heat[..., :-1] * warmth_fringe[1:-1, 1:-1, :-2] + col_heat[..., 1:] * warmth_fringe[1:-1, 1:-1, 2:]
        final_warmth = inward_current_flow / overall_total
    leftover_energy = observed_energy(probe_weighting, final_warmth)
    updated_admittance = baseline_admittance[metal_category] / (1.0 + thermal_slope * leftover_energy)
    return voltage_loss, final_warmth, updated_admittance
```

```python
import jax
import jax.numpy as jnp
from jax import lax
from jax.sharding import PartitionSpec as P

SWEEPS = 4


shunt_level = 0.05
pad_conductance = 4.0
via_conductance = 2.0
thermal_slope = 0.2
sink_level = 0.1


def extended(value, sides, width):
    for axis, dim in sides:
        devices, length = (lax.axis_size(axis), value.shape[dim])
        up = [(i, (i + 1) % devices) for i in range(devices - 1)]
        down = [(j, i) for i, j in up]
        last = lax.slice_in_dim(value, length - width, length, axis=dim)
        initial = lax.slice_in_dim(value, 0, width, axis=dim)
        before = lax.ppermute(last, axis, up)
        after = lax.ppermute(initial, axis, down)
        value = jnp.concatenate([before, value, after], axis=dim)
    return value


def harmonic(first, second):
    return first * second / (first + second)


def layer_rim(stacked):
    return extended(stacked, (("tile", 2), ("therm", 1)), 1)


def block_fringe(stacked):
    return extended(stacked, (("tile", 2), ("therm", 1)), 1)


def class_table(baseline_admittance, metal_category):
    table = jnp.zeros(metal_category.shape, jnp.float32)
    for number in range(baseline_admittance.shape[0]):
        table = table + jnp.where(metal_category == number, baseline_admittance[number], 0.0)
    return table


def swap(value, axis, bit):
    return lax.ppermute(value, axis, [(i, i ^ bit) for i in range(lax.axis_size(axis))])


def ohmic_warming(probe_weighting, field, owned_strata, stratum_shift):
    present_stratum = field.shape[0]
    weights = lax.dynamic_slice(
        probe_weighting,
        (0, stratum_shift),
        (owned_strata * lax.axis_size("therm"), present_stratum),
    )
    place = lax.axis_index("therm")
    part = jnp.einsum("lz,zxy->lxy", weights, field, precision=lax.Precision.HIGHEST)
    part = part.reshape((2, 2, owned_strata) + part.shape[1:])
    core, far = place % 2, place // 2
    mine = lax.dynamic_index_in_dim(part, core, 1, False)
    other = lax.dynamic_index_in_dim(part, 1 - core, 1, False)
    pair = mine + swap(other, "therm", 1)
    mine = lax.dynamic_index_in_dim(pair, far, 0, False)
    other = lax.dynamic_index_in_dim(pair, 1 - far, 0, False)
    return mine + swap(other, "therm", 2)


def gather_layers(power):
    place = lax.axis_index("therm")
    core, far = place % 2, place // 2
    other = swap(power, "therm", 2)
    pair = jnp.stack([power, other])
    pair = jnp.where(far == 0, pair, pair[::-1])
    mate = swap(pair, "therm", 1)
    both = jnp.where(core == 0, jnp.stack([pair, mate], 1), jnp.stack([mate, pair], 1))
    return both.reshape((-1,) + power.shape[1:])


def total_of(values):
    for axis, bit in (("therm", 1), ("therm", 2), ("tile", 1), ("tile", 2), ("tile", 4), ("tile", 8), ("tile", 16)):
        values = values + swap(values, axis, bit)
    return values


def coefficients(moments):
    m1, m2, m3, m4, m5 = [moments[k] / moments[0] for k in range(1, 6)]
    s0, s1, s2 = lax.rsqrt(m1), lax.rsqrt(m3), lax.rsqrt(m5)
    n10, n20, n21 = m2 * s0 * s1, m3 * s0 * s2, m4 * s1 * s2
    g0, g1, g2 = s0, m1 * s1, m2 * s2
    d1 = 1.0 - n10 * n10
    ok1 = d1 > 1e-6
    y1 = g1 - n10 * g0
    t = n21 - n20 * n10
    l21 = jnp.where(ok1, t / jnp.where(ok1, d1, 1.0), 0.0)
    d2 = 1.0 - n20 * n20 - l21 * t
    ok2 = ok1 & (d2 > 1e-6)
    y2 = g2 - n20 * g0 - l21 * y1
    c2 = jnp.where(ok2, y2 / jnp.where(ok2, d2, 1.0), 0.0)
    c1 = jnp.where(ok1, y1 / jnp.where(ok1, d1, 1.0), 0.0) - l21 * c2
    c0 = g0 - n10 * c1 - n20 * c2
    return c0 * s0 / 16.0, c1 * s1 / 16.0, c2 * s2 / 16.0


def beside(field):
    tiles, therms = lax.axis_size("tile"), lax.axis_size("therm")
    def move(value, axis, n, step):
        return lax.ppermute(value, axis, [(i, i + step) for i in range(n) if 0 <= i + step < n])
    return (
        move(field[:, -1:], "tile", tiles, 1),
        move(field[:, :1], "tile", tiles, -1),
        move(field[-1:], "therm", therms, 1),
        move(field[:1], "therm", therms, -1),
    )


def contact_stripes(field):
    return jnp.pad(field, ((0, 0), (0, 0), (1, 1)))


def per_device(
    sink_current,
    metal_category,
    upward_link_flag,
    supply_contact_flag,
    baseline_admittance,
    beginning_warmth,
    cell_diffusivity,
    dissipation_split,
    probe_weighting,
):
    owned_strata = sink_current.shape[0]
    present_stratum = beginning_warmth.shape[0]
    stratum_shift = lax.axis_index("therm") * present_stratum
    table = class_table(baseline_admittance, metal_category)
    power_density = ohmic_warming(probe_weighting, beginning_warmth, owned_strata, stratum_shift)
    lateral = table / (1.0 + thermal_slope * power_density)
    vertical = (
        upward_link_flag.astype(jnp.float32)
        * via_conductance
        / (1.0 + thermal_slope * power_density)
    )
    grounded = shunt_level + supply_contact_flag.astype(jnp.float32) * pad_conductance
    rimmed = layer_rim(jnp.stack([lateral, vertical]))
    lateral_rim = rimmed[0]
    below = rimmed[1][:-2, 1:-1, :]
    row_edges = harmonic(lateral_rim[1:-1, :-1, :], lateral_rim[1:-1, 1:, :])
    lateral_cols = contact_stripes(lateral)
    col_edges = harmonic(lateral_cols[..., :-1], lateral_cols[..., 1:])
    diagonal = (
        grounded
        + vertical
        + below
        + row_edges[:, :-1]
        + row_edges[:, 1:]
        + col_edges[..., :-1]
        + col_edges[..., 1:]
    )

    def surround(field, sides):
        up, down, under, over = sides
        rows = jnp.concatenate([up, field, down], 1)
        layers = jnp.concatenate([under, field, over], 0)
        return rows, layers, contact_stripes(field)

    def neighbours(around):
        rows, layers, cols = around
        return (rows[:, :-2], rows[:, 2:], cols[..., :-2], cols[..., 2:], layers[2:], layers[:-2])

    edges = (row_edges[:, :-1], row_edges[:, 1:], col_edges[..., :-1], col_edges[..., 1:], vertical, below)

    def operate(field, around):
        result = diagonal * field
        for edge, far in zip(edges, neighbours(around)):
            result = result - edge * far
        return result * 0.0625

    sides0 = beside(sink_current)
    around0 = surround(sink_current, sides0)
    first = operate(sink_current, around0)
    sides1 = beside(first)
    around1 = surround(first, sides1)
    second = operate(first, around1)
    sides2 = beside(second)
    around2 = surround(second, sides2)
    third = operate(second, around2)
    moments = total_of(
        jnp.stack(
            [
                jnp.sum(sink_current * sink_current),
                jnp.sum(sink_current * first),
                jnp.sum(first * first),
                jnp.sum(first * second),
                jnp.sum(second * second),
                jnp.sum(second * third),
            ]
        )
    )
    c0, c1, c2 = coefficients(moments)
    voltage_loss = c0 * sink_current + c1 * first + c2 * second
    around = surround(
        voltage_loss, [c0 * p + c1 * q + c2 * r for p, q, r in zip(sides0, sides1, sides2)]
    )
    pairs = zip(edges, neighbours(around))
    edge_power = jnp.zeros_like(voltage_loss)
    for edge, other in pairs:
        edge_power = edge_power + edge * (voltage_loss - other) * (voltage_loss - other)
    power = grounded * voltage_loss * voltage_loss + 0.5 * edge_power
    piece = gather_layers(power)
    weights = lax.dynamic_slice(
        dissipation_split, (stratum_shift, 0), (present_stratum, piece.shape[0])
    )
    source = jnp.einsum("zl,lxy->zxy", weights, piece, precision=lax.Precision.HIGHEST)
    krim = block_fringe(cell_diffusivity[None])[0]
    depth_edges = harmonic(krim[:-1, 1:-1, :], krim[1:, 1:-1, :])
    row_heat = harmonic(krim[1:-1, :-1, :], krim[1:-1, 1:, :])
    kcols = contact_stripes(cell_diffusivity)
    col_heat = harmonic(kcols[..., :-1], kcols[..., 1:])
    overall_total = (
        sink_level
        + depth_edges[:-1]
        + depth_edges[1:]
        + row_heat[:, :-1]
        + row_heat[:, 1:]
        + col_heat[..., :-1]
        + col_heat[..., 1:]
    )
    final_warmth = beginning_warmth
    for sweep in range(SWEEPS):
        up, down, under, over = beside(final_warmth)
        rows = jnp.concatenate([up, final_warmth, down], 1)
        layers = jnp.concatenate([under, final_warmth, over], 0)
        cols = contact_stripes(final_warmth)
        inward_current_flow = (
            source
            + depth_edges[:-1] * layers[:-2]
            + depth_edges[1:] * layers[2:]
        )
        inward_current_flow = (
            inward_current_flow
            + row_heat[:, :-1] * rows[:, :-2]
            + row_heat[:, 1:] * rows[:, 2:]
        )
        inward_current_flow = (
            inward_current_flow
            + col_heat[..., :-1] * cols[..., :-2]
            + col_heat[..., 1:] * cols[..., 2:]
        )
        final_warmth = inward_current_flow / overall_total
    leftover_energy = ohmic_warming(probe_weighting, final_warmth, owned_strata, stratum_shift)
    updated_admittance = table / (1.0 + thermal_slope * leftover_energy)
    return (voltage_loss, final_warmth, updated_admittance)


def solution(mesh):
    return jax.shard_map(
        per_device,
        mesh=mesh,
        in_specs=(
            P("therm", "tile", None),
            P("therm", "tile", None),
            P("therm", "tile", None),
            P("therm", "tile", None),
            P(),
            P("therm", "tile", None),
            P("therm", "tile", None),
            P(),
            P(),
        ),
        out_specs=(P("therm", "tile", None), P("therm", "tile", None), P("therm", "tile", None)),
        check_vma=False,
    )
```

```python
import functools

import jax
import jax.numpy as jnp
from jax import lax
from jax.experimental import pallas as pl
from jax.experimental.pallas import tpu as pltpu
from jax.sharding import PartitionSpec as P


LAYERS = 12
HALF = LAYERS // 2
OWN = 3
DEPTHS = 64
SLAB = DEPTHS // 2
DEEP = 16
ROWS = 16
RIM = 3
EXT = ROWS + 2 * RIM
HEATED = 7
SWEEPS = 4
WIDE = ROWS + 2 * SWEEPS
THICK = SLAB + SWEEPS
SCALE = 1.0 / 16.0
TINY = 1e-30

shunt_level = 0.05
pad_conductance = 4.0
via_conductance = 2.0
thermal_slope = 0.2
sink_level = 0.1

F32 = jnp.float32


def place():
    therm = lax.axis_index("therm")
    return therm // 2, therm % 2


def tile_spec(n):
    return [pl.BlockSpec(memory_space=pltpu.VMEM)] * n


def shaped(*dims):
    return jax.ShapeDtypeStruct(dims + (8, 128), F32)


def call(kernel, outs, scratch=(), scalars=0, cost=0):
    def run(*args):
        smem = [pl.BlockSpec(memory_space=pltpu.SMEM)] * scalars
        return pl.pallas_call(
            kernel,
            out_shape=outs,
            in_specs=smem + tile_spec(len(args) - scalars),
            out_specs=jax.tree.map(lambda _: pl.BlockSpec(memory_space=pltpu.VMEM), outs),
            scratch_shapes=[pltpu.VMEM(dims + (8, 128), F32) for dims in scratch],
            compiler_params=pltpu.CompilerParams(vmem_limit_bytes=56 * 1024 * 1024),
            cost_estimate=pl.CostEstimate(flops=cost * 2000, bytes_accessed=cost * 3000, transcendentals=0),
        )(*args)

    return run


def raw_view(value):
    n, rows, width = value.shape
    split = value.reshape(n, rows // 8, 8, width // 128, 128).transpose(0, 1, 3, 2, 4)
    return split.reshape(n, rows // 8, 8 * (width // 128), 128)


def raw_back(value):
    n, blocks, high, lanes = value.shape
    split = value.reshape(n, blocks, high // 8, 8, lanes).transpose(0, 1, 3, 2, 4)
    return split.reshape(n, blocks * 8, (high // 8) * lanes)


def at_row(ref, n, chunk, row):
    return ref[n, chunk * 2 + row // 8, pl.ds(row % 8, 8, stride=8), :]


def loop(count, body):
    def step(i, carry):
        body(i)
        return carry

    lax.fori_loop(0, count, step, 0)


def iotas():
    return lax.broadcasted_iota(jnp.int32, (8, 128), 0), lax.broadcasted_iota(jnp.int32, (8, 128), 1)


def after(v, lane):
    r = pltpu.roll(v, 127, 1)
    return jnp.where(lane == 127, pltpu.roll(r, 7, 0), r)


def before(v, lane):
    r = pltpu.roll(v, 1, 1)
    return jnp.where(lane == 0, pltpu.roll(r, 1, 0), r)


def inverse(v):
    r = pl.reciprocal(v, approx=True)
    r = r * (2.0 - v * r)
    return r * (2.0 - v * r)


def harmonic(a, b):
    return a * b * inverse(jnp.maximum(a + b, TINY))


def pack_kernel(value, own, send):
    _, core = place()

    def body(n):
        for row in range(ROWS):
            own[n, row] = at_row(value, n, core, row)
            send[n, row] = at_row(value, n, 1 - core, row)

    loop(value.shape[0], body)


def pack_args_kernel(classes, sink, category, link, contact, own, send):
    _, core = place()

    def body(n):
        for row in range(ROWS):
            for chunk, out in ((core, own), (1 - core, send)):
                kind = at_row(category, n, chunk, row)
                table = jnp.full((8, 128), classes[0], F32)
                for number in range(1, 8):
                    table = jnp.where(kind == number, classes[number], table)
                out[n, row] = at_row(sink, n, chunk, row)
                out[OWN + n, row] = table * SCALE
                out[2 * OWN + n, row] = at_row(link, n, chunk, row).astype(F32) * (via_conductance * SCALE)
                out[3 * OWN + n, row] = at_row(contact, n, chunk, row).astype(F32) * (
                    pad_conductance * SCALE
                ) + (shunt_level * SCALE)

    loop(OWN, body)


def weigh(weights, stride, parts, acc):
    def rows(block):
        total = [jnp.zeros((8, 128), F32)] * (4 * LAYERS)
        for ref, first, base in parts:

            def step(z, total):
                field = [ref[first + z, block * 4 + k] for k in range(4)]
                out = []
                for layer in range(LAYERS):
                    w = weights[layer * stride + base + z]
                    out += [total[layer * 4 + k] + w * field[k] for k in range(4)]
                return tuple(out)

            total = lax.fori_loop(0, DEEP, step, tuple(total), unroll=4)
        for layer in range(LAYERS):
            for k in range(4):
                acc[layer, block * 4 + k] = total[layer * 4 + k]

    loop(ROWS // 4, rows)


def heat_kernel(weights, t_own, t_got, a_own, a_got, part, a6, s_far, s_core_far, s_tile_far, s_core, s_tile):
    far, core = place()
    weigh(
        weights,
        DEPTHS,
        ((t_own, 0, SLAB * far + DEEP * core), (t_got, 0, SLAB * far + DEEP * (1 - core))),
        part,
    )

    def merge(n):
        for row in range(ROWS):
            for ch in range(4):
                a6[ch, OWN * core + n, row] = a_own[ch * OWN + n, row]
                a6[ch, OWN * (1 - core) + n, row] = a_got[ch * OWN + n, row]

    loop(OWN, merge)
    to_core, to_tile = (ROWS - RIM) * (1 - core), (ROWS - RIM) * core

    def heats(n):
        for row in range(ROWS):
            s_far[n, row] = part[5 * (1 - far) + n, row]
        for k in range(RIM):
            s_core_far[n, k] = part[5 * (1 - far) + n, to_core + k]
            s_tile_far[n, k] = part[5 * (1 - far) + n, to_tile + k]
            s_core[n, k] = part[5 * far + n, to_core + k]
            s_tile[n, k] = part[5 * far + n, to_tile + k]

    loop(HEATED, heats)
    edge = 5 * (1 - far)
    for n, ch in ((HEATED, 0), (HEATED + 1, 2)):
        for row in range(ROWS):
            s_far[n, row] = a6[ch, edge, row]
        for k in range(RIM):
            s_core_far[n, k] = a6[ch, edge, to_core + k]
            s_tile_far[n, k] = a6[ch, edge, to_tile + k]

    def args(o):
        for ch in range(4):
            for k in range(RIM):
                s_core[HEATED + ch * HALF + o, k] = a6[ch, o, to_core + k]
                s_tile[HEATED + ch * HALF + o, k] = a6[ch, o, to_tile + k]

    loop(HALF, args)


def apply(v, o, row, diag, row_edge, col_edge, vert, lane):
    here = v[o + 1, row]
    ce = col_edge[o, row]
    return (
        diag[o, row] * here
        - row_edge[o, row - 1] * v[o + 1, row - 1]
        - row_edge[o, row] * v[o + 1, row + 1]
        - ce * after(here, lane)
        - before(ce * here, lane)
        - vert[o + 1, row] * v[o + 2, row]
        - vert[o, row] * v[o, row]
    )


def basis_kernel(
    part, a6, g_far, g_core_far, g_tile_far, g_core, g_tile,
    v0, v1, v2, diag, row_edge, col_edge, vert, ground, s_basis, inv, lat,
):
    far, core = place()
    sub, lane = iotas()
    from_core, from_tile = (EXT - RIM) * (1 - core), (EXT - RIM) * core
    zero = jnp.zeros((8, 128), F32)

    def heats(n):
        def one(row, heat):
            inv[n, row] = inverse(1.0 + thermal_slope * heat)

        for k in range(ROWS):
            one(RIM + k, part[5 * far + n, k] + g_far[n, k])
        for k in range(RIM):
            one(from_core + k, g_core[n, k] + g_core_far[n, k])
            one(from_tile + k, g_tile[n, k] + g_tile_far[n, k])

    loop(HEATED, heats)
    lower = far.astype(F32)
    halo, none = 7 * (1 - far), 7 * far

    def rim(row, b, up):
        v0[halo, row] = b
        v0[none, row] = zero
        vert[0, row] = up * inv[0, row] * lower

    for k in range(ROWS):
        rim(RIM + k, g_far[HEATED, k], g_far[HEATED + 1, k])
    for k in range(RIM):
        rim(from_core + k, g_core_far[HEATED, k], g_core_far[HEATED + 1, k])
        rim(from_tile + k, g_tile_far[HEATED, k], g_tile_far[HEATED + 1, k])
    for row in range(EXT):
        for edge in (0, 7):
            v1[edge, row] = zero
            v2[edge, row] = zero

    def fields(o):
        def one(row, b, g, up, gr):
            warm = inv[o + far, row]
            v0[o + 1, row] = b
            lat[o, row] = g * warm
            vert[o + 1, row] = up * warm
            ground[o, row] = gr

        for k in range(ROWS):
            one(RIM + k, *[a6[ch, o, k] for ch in range(4)])
        for k in range(RIM):
            one(from_core + k, *[g_core[HEATED + ch * HALF + o, k] for ch in range(4)])
            one(from_tile + k, *[g_tile[HEATED + ch * HALF + o, k] for ch in range(4)])

    loop(HALF, fields)
    last = (sub == 7) & (lane == 127)

    def edges(o):
        for row in range(EXT - 1):
            row_edge[o, row] = harmonic(lat[o, row], lat[o, row + 1])
        for row in range(1, EXT - 1):
            here = lat[o, row]
            ce = jnp.where(last, 0.0, harmonic(here, after(here, lane)))
            col_edge[o, row] = ce
            diag[o, row] = (
                ground[o, row] + vert[o + 1, row] + vert[o, row]
                + row_edge[o, row - 1] + row_edge[o, row] + ce + before(ce, lane)
            )

    loop(HALF, edges)

    def first(o):
        for row in range(1, EXT - 1):
            v1[o + 1, row] = apply(v0, o, row, diag, row_edge, col_edge, vert, lane)

    loop(HALF, first)

    def second(o):
        for row in range(2, EXT - 2):
            v2[o + 1, row] = apply(v1, o, row, diag, row_edge, col_edge, vert, lane)

    loop(HALF, second)
    edge = 5 * (1 - far) + 1
    for k in range(EXT - 4):
        s_basis[0, k] = v1[edge, 2 + k]
        s_basis[1, k] = v2[edge, 2 + k]


def moments_kernel(v0, v1, v2, diag, row_edge, col_edge, vert, got, w2, out):
    far, _ = place()
    _, lane = iotas()

    def copy(n):
        for row in range(2, EXT - 2):
            w2[n, row] = v2[n, row]

    loop(HALF + 2, copy)
    edge, halo = 5 * (1 - far) + 1, 7 * (1 - far)
    for k in range(EXT - 4):
        row = 2 + k
        link = vert[6 * (1 - far), row]
        w2[edge, row] = v2[edge, row] - link * got[0, k]
        w2[halo, row] = got[1, k] - link * v1[edge, row]

    def body(o, sums):
        sums = list(sums)
        for row in range(RIM, RIM + ROWS):
            a, b, c = v0[o + 1, row], v1[o + 1, row], w2[o + 1, row]
            d = apply(w2, o, row, diag, row_edge, col_edge, vert, lane)
            for n, term in enumerate((a * a, a * b, b * b, b * c, c * c, c * d)):
                sums[n] = sums[n] + term
        return tuple(sums)

    sums = lax.fori_loop(0, HALF, body, (jnp.zeros((8, 128), F32),) * 6)
    for n in range(6):
        out[0, pl.ds(n, 1), :] = jnp.full((1, 128), jnp.sum(sums[n]), F32)
    out[0, pl.ds(6, 2), :] = jnp.zeros((2, 128), F32)
    out[1] = jnp.zeros((8, 128), F32)


def two_sum(a, b):
    s = a + b
    t = s - a
    return s, (a - (s - t)) + (b - t)


def two_prod(a, b):
    def split(v):
        t = v * 4097.0
        high = t - (t - v)
        return high, v - high

    p = a * b
    (ah, al), (bh, bl) = split(a), split(b)
    return p, ((ah * bh - p) + ah * bl + al * bh) + al * bl


def pair_add(a, b):
    s, e = two_sum(a[0], b[0])
    e = e + (a[1] + b[1])
    high = s + e
    return high, e - (high - s)


def pair_mul(a, b):
    p, e = two_prod(a[0], b[0])
    e = e + (a[0] * b[1] + a[1] * b[0])
    high = p + e
    return high, e - (high - p)


def pair_neg(a):
    return -a[0], -a[1]


def pair_div(a, b):
    q = a[0] / b[0]
    r = pair_add(a, pair_neg(pair_mul(b, (q, jnp.zeros_like(q)))))
    q2 = (r[0] + r[1]) / b[0]
    high = q + q2
    return high, q2 - (high - q)


def coefficients(m):
    mean, m2, m3, m4, m5 = [pair_div(v, m[0]) for v in m[1:]]
    low = pair_neg(mean)

    def lowered(seq):
        return [pair_add(b, pair_mul(low, a)) for a, b in zip(seq, seq[1:])]

    one = (jnp.ones_like(mean[0]), jnp.zeros_like(mean[0]))
    seq = [one, mean, m2, m3, m4, m5]
    seq = lowered(seq)
    central = []
    for power in range(2, 6):
        seq = lowered(seq)
        central.append(seq[0])
    c2, c3, c4, c5 = [v[0] + v[1] for v in central]
    s = mean[0] + mean[1]
    ok1 = c2 > 3e-8 * s * s
    c2 = jnp.where(ok1, c2, 1.0)
    skew = c3 / c2
    n2 = c4 - skew * c3 - c2 * c2
    ok2 = ok1 & (n2 > 1e-6 * c2 * c2) & (n2 > 3e-8 * (s * s) * (s * s))
    n2 = jnp.where(ok2, n2, 1.0)
    tq = c5 - 2.0 * skew * c4 + (skew * skew - 2.0 * c2) * c3 + 2.0 * skew * c2 * c2
    a2 = s + tq / n2
    a1 = s + skew
    b1, b2 = c2, n2 / c2
    d0 = s
    d1 = a1 - b1 / d0
    d2 = a2 - b2 / d1
    y0 = 1.0 / d0
    y1 = jnp.where(ok1, -y0 / d1, 0.0)
    y2 = jnp.where(ok2, -y1 / d2, 0.0)
    z2 = y2
    z1 = y1 - jnp.where(ok2, b2 * z2 / d1, 0.0)
    z0 = y0 - jnp.where(ok1, b1 * z1 / d0, 0.0)
    k2 = z2
    k1 = z1 - z2 * (skew + 2.0 * s)
    k0 = z0 - z1 * s + z2 * (s * s + skew * s - c2)
    return k0 * SCALE, k1 * SCALE, k2 * SCALE


def power_kernel(
    total, v0, v1, w2, diag, row_edge, col_edge, vert, ground, got,
    power, s_core, s_tile, loss, s_loss, volts,
):
    far, core = place()
    _, lane = iotas()
    spread = [
        (
            jnp.broadcast_to(total[0, pl.ds(n, 1), :], (8, 128)),
            jnp.broadcast_to(total[1, pl.ds(n, 1), :], (8, 128)),
        )
        for n in range(6)
    ]
    c0, c1, c2 = coefficients(spread)
    halo = 7 * (1 - far)

    def combine(n):
        for row in range(2, EXT - 2):
            volts[n, row] = c0 * v0[n, row] + c1 * v1[n, row] + c2 * w2[n, row]

    loop(HALF + 2, combine)
    for k in range(EXT - 4):
        row = 2 + k
        volts[halo, row] = c0 * v0[halo, row] + c1 * got[0, k] + c2 * w2[halo, row]

    def body(o):
        for k in range(ROWS):
            row = RIM + k
            x = volts[o + 1, row]
            near = after(x, lane) - x
            q = col_edge[o, row] * near * near
            q = q + before(q, lane)
            for edge, other in (
                (row_edge[o, row - 1], volts[o + 1, row - 1]),
                (row_edge[o, row], volts[o + 1, row + 1]),
                (vert[o + 1, row], volts[o + 2, row]),
                (vert[o, row], volts[o, row]),
            ):
                d = x - other
                q = q + edge * d * d
            power[o, k] = 16.0 * ground[o, row] * x * x + 8.0 * q

    loop(HALF, body)
    to_core, to_tile = (ROWS - RIM) * (1 - core), (ROWS - RIM) * core

    def sides(o):
        for k in range(RIM):
            s_core[o, k] = power[o, to_core + k]
            s_tile[o, k] = power[o, to_tile + k]

    loop(HALF, sides)

    def outs(n):
        for k in range(ROWS):
            loss[n, k] = volts[1 + OWN * core + n, RIM + k]
            s_loss[n, k] = volts[1 + OWN * (1 - core) + n, RIM + k]

    loop(OWN, outs)


def slab_rim_kernel(t_own, t_got, k_own, k_got, s_core, s_tile):
    _, core = place()
    to_core, to_tile = (ROWS - SWEEPS) * (1 - core), (ROWS - SWEEPS) * core

    def body(n):
        for f, (own, got) in enumerate(((t_own, t_got), (k_own, k_got))):
            for ref, z in ((own, DEEP * core + n), (got, DEEP * (1 - core) + n)):
                for k in range(SWEEPS):
                    s_core[f, z, k] = ref[n, to_core + k]
                    s_tile[f, z, k] = ref[n, to_tile + k]

    loop(DEEP, body)


def slab_wide_kernel(t_own, t_got, k_own, k_got, g_core, g_tile, wide, s_far):
    far, core = place()
    from_core, from_tile = (WIDE - SWEEPS) * (1 - core), (WIDE - SWEEPS) * core

    def body(n):
        for f, (own, got) in enumerate(((t_own, t_got), (k_own, k_got))):
            for ref, z in ((own, DEEP * core + n), (got, DEEP * (1 - core) + n)):
                for k in range(ROWS):
                    wide[f, z, SWEEPS + k] = ref[n, k]
                for k in range(SWEEPS):
                    wide[f, z, from_core + k] = g_core[f, z, k]
                    wide[f, z, from_tile + k] = g_tile[f, z, k]

    loop(DEEP, body)
    first = (SLAB - SWEEPS) * (1 - far)

    def send(n):
        for f in range(2):
            for row in range(WIDE):
                s_far[f, n, row] = wide[f, first + n, row]

    loop(SWEEPS, send)


def slab_edges_kernel(wide, g_far, warm, deep_edge, row_edge, col_edge, turn, cond):
    far, _ = place()
    sub, lane = iotas()
    zero = jnp.zeros((8, 128), F32)

    def body(n):
        for row in range(WIDE):
            warm[1 + SWEEPS * far + n, row] = wide[0, n, row]
            cond[SWEEPS * far + n, row] = wide[1, n, row]

    loop(SLAB, body)

    def rim(n):
        for row in range(WIDE):
            warm[1 + SLAB * (1 - far) + n, row] = g_far[0, n, row]
            cond[SLAB * (1 - far) + n, row] = g_far[1, n, row]

    loop(SWEEPS, rim)
    for row in range(WIDE):
        for n in (0, THICK + 1):
            warm[n, row] = zero
        for n in (0, THICK):
            deep_edge[n, row] = zero

    def deep(n):
        for row in range(WIDE):
            deep_edge[n + 1, row] = harmonic(cond[n, row], cond[n + 1, row])

    loop(THICK - 1, deep)
    last = (sub == 7) & (lane == 127)

    def edges(n):
        for row in range(WIDE - 1):
            row_edge[n, row] = harmonic(cond[n, row], cond[n, row + 1])
        for row in range(1, WIDE - 1):
            here = cond[n, row]
            ce = jnp.where(last, 0.0, harmonic(here, after(here, lane)))
            col_edge[n, row] = ce
            turn[n, row] = inverse(
                sink_level + deep_edge[n, row] + deep_edge[n + 1, row]
                + row_edge[n, row - 1] + row_edge[n, row] + ce + before(ce, lane)
            )

    loop(THICK, edges)


def sweeps_kernel(
    split, weights, power, p_far, p_core, p_core_far, p_tile, p_tile_far,
    warm, deep_edge, row_edge, col_edge, turn,
    out, s_out, final, s_final,
    joule, source, one, two,
):
    far, core = place()
    _, lane = iotas()
    zero = jnp.zeros((8, 128), F32)
    from_core = 1 + (EXT - RIM) * (1 - core)
    from_tile = 1 + (EXT - RIM) * core

    def gather(o):
        for layer, mid, by_core, by_tile in (
            (HALF * far + o, power, p_core, p_tile),
            (HALF * (1 - far) + o, p_far, p_core_far, p_tile_far),
        ):
            for k in range(ROWS):
                joule[layer, SWEEPS + k] = mid[o, k]
            for k in range(RIM):
                joule[layer, from_core + k] = by_core[o, k]
                joule[layer, from_tile + k] = by_tile[o, k]
            joule[layer, 0] = zero
            joule[layer, WIDE - 1] = zero

    loop(HALF, gather)
    base = (SLAB - SWEEPS) * far

    def sources(block):
        field = [[joule[layer, block * 4 + k] for k in range(4)] for layer in range(LAYERS)]

        def depth(n, carry):
            total = [zero] * 4
            for layer in range(LAYERS):
                w = split[(base + n) * LAYERS + layer]
                total = [total[k] + w * field[layer][k] for k in range(4)]
            for k in range(4):
                source[n, block * 4 + k] = total[k]
            return carry

        lax.fori_loop(0, THICK, depth, 0)

    loop(WIDE // 4, sources)
    for ref in (one, two):
        for row in range(WIDE):
            ref[0, row] = zero
            ref[THICK + 1, row] = zero

    before_ref = warm
    for sweep in range(1, SWEEPS + 1):
        after_ref = one if sweep % 2 else two
        start = sweep * far

        def step(i, src=before_ref, dst=after_ref, sweep=sweep, start=start):
            n = start + i
            for row in range(sweep, WIDE - sweep):
                here = src[n + 1, row]
                ce = col_edge[n, row]
                flow = source[n, row] + ce * after(here, lane) + before(ce * here, lane)
                flow = flow + row_edge[n, row - 1] * src[n + 1, row - 1] + row_edge[n, row] * src[n + 1, row + 1]
                flow = flow + deep_edge[n, row] * src[n, row] + deep_edge[n + 1, row] * src[n + 2, row]
                dst[n + 1, row] = flow * turn[n, row]

        loop(THICK - sweep, step)
        before_ref = after_ref

    def outs(n):
        for k in range(ROWS):
            out[n, k] = before_ref[1 + SWEEPS * far + DEEP * core + n, SWEEPS + k]
            s_out[n, k] = before_ref[1 + SWEEPS * far + DEEP * (1 - core) + n, SWEEPS + k]

    loop(DEEP, outs)
    weigh(
        weights,
        DEPTHS,
        ((out, 0, SLAB * far + DEEP * core), (s_out, 0, SLAB * far + DEEP * (1 - core))),
        final,
    )

    def sends(o):
        for k in range(ROWS):
            s_final[o, k] = final[HALF * (1 - far) + o, k]

    loop(HALF, sends)


def update_kernel(final, got, a6, mine, send):
    far, core = place()

    def body(n):
        for half, out in ((core, mine), (1 - core, send)):
            o = OWN * half + n
            for k in range(ROWS):
                heat = final[HALF * far + o, k] + got[o, k]
                out[n, k] = (16.0 * a6[1, o, k]) * inverse(1.0 + thermal_slope * heat)

    loop(OWN, body)


def unpack_kernel(own, got, out):
    _, core = place()

    def body(n):
        for k in range(ROWS):
            out[n, core * 2 + k // 8, pl.ds(k % 8, 8, stride=8), :] = own[n, k]
            out[n, (1 - core) * 2 + k // 8, pl.ds(k % 8, 8, stride=8), :] = got[n, k]

    loop(own.shape[0], body)


def unpack(own, got):
    n = own.shape[0]
    out = jax.ShapeDtypeStruct((n, 4, 64, 128), F32)
    return raw_back(call(unpack_kernel, out, cost=n)(own, got))


def pack(value):
    n = value.shape[0]
    return call(pack_kernel, [shaped(n, ROWS)] * 2, cost=n)(raw_view(value))


def to_core(value):
    return lax.ppermute(value, "therm", [(i, i ^ 1) for i in range(4)])


def to_far(value):
    return lax.ppermute(value, "therm", [(i, i ^ 2) for i in range(4)])


def to_core_far(value):
    return lax.ppermute(value, "therm", [(i, i ^ 3) for i in range(4)])


def to_tile(value, cross=0):
    pairs = []
    for t in range(lax.axis_size("tile") - 1):
        for half in range(2):
            low = 4 * t + 2 * half + 1
            high = 4 * (t + 1) + 2 * (half ^ cross)
            pairs += [(low, high), (high, low)]
    return lax.ppermute(value, ("tile", "therm"), pairs)


def total_of(values):
    def add(a, b):
        high, low = pair_add((a[0], a[1]), (b[0], b[1]))
        return jnp.stack([high, low])

    values = add(values, to_core(values))
    x_peers = []
    for bits in (1, 2, 3):
        pairs = []
        for t in range(lax.axis_size("tile")):
            for h in range(4):
                pairs.append((4 * t + h, 4 * (t ^ (bits & 1)) + (h ^ (bits & 2))))
        x_peers.append(lax.ppermute(values, ("tile", "therm"), pairs))
    for peer in x_peers:
        values = add(values, peer)
    for unit in (2, 8):
        peers = [
            lax.ppermute(values, "tile", [(t, t ^ (unit * k)) for t in range(lax.axis_size("tile"))])
            for k in (1, 2, 3)
        ]
        for peer in peers:
            values = add(values, peer)
    return values


def per_device(
    sink_current,
    metal_category,
    upward_link_flag,
    supply_contact_flag,
    baseline_admittance,
    beginning_warmth,
    cell_diffusivity,
    dissipation_split,
    probe_weighting,
):
    weights = probe_weighting.reshape(-1)
    split = dissipation_split.reshape(-1)
    t_own, t_send = pack(beginning_warmth)
    t_got = to_core(t_send)
    a_own, a_send = call(pack_args_kernel, [shaped(4 * OWN, ROWS)] * 2, scalars=1, cost=12)(
        baseline_admittance,
        *[raw_view(v) for v in (sink_current, metal_category, upward_link_flag, supply_contact_flag)],
    )
    a_got = to_core(a_send)
    k_own, k_send = pack(cell_diffusivity)
    k_got = to_core(k_send)

    part, a6, s_far, s_core_far, s_tile_far, s_core, s_tile = call(
        heat_kernel,
        [
            shaped(LAYERS, ROWS),
            shaped(4, HALF, ROWS),
            shaped(HEATED + 2, ROWS),
            shaped(HEATED + 2, RIM),
            shaped(HEATED + 2, RIM),
            shaped(HEATED + 4 * HALF, RIM),
            shaped(HEATED + 4 * HALF, RIM),
        ],
        scalars=1,
        cost=24,
    )(weights, t_own, t_got, a_own, a_got)
    g_far = to_far(s_far)
    g_tile = to_tile(s_tile)
    g_tile_far = to_tile(s_tile_far, 1)
    g_core_far = to_core_far(s_core_far)
    g_core = to_core(s_core)

    field = shaped(HALF + 2, EXT)
    coef = shaped(HALF, EXT)
    v0, v1, v2, diag, row_edge, col_edge, vert, ground, s_basis = call(
        basis_kernel,
        [field, field, field, coef, coef, coef, shaped(HALF + 1, EXT), coef, shaped(2, EXT - 4)],
        scratch=((HEATED, EXT), (HALF, EXT)),
        cost=16,
    )(part, a6, g_far, g_core_far, g_tile_far, g_core, g_tile)
    g_basis = to_far(s_basis)
    w2, sums = call(moments_kernel, [field, shaped(2)], cost=10)(
        v0, v1, v2, diag, row_edge, col_edge, vert, g_basis
    )
    total = total_of(sums)

    rim = shaped(2, SLAB, SWEEPS)
    k_core, k_tile = call(slab_rim_kernel, [rim, rim], cost=8)(t_own, t_got, k_own, k_got)
    wide, s_deep = call(slab_wide_kernel, [shaped(2, SLAB, WIDE), shaped(2, SWEEPS, WIDE)], cost=24)(
        t_own, t_got, k_own, k_got, to_core(k_core), to_tile(k_tile)
    )
    thick = shaped(THICK, WIDE)
    warm, deep_edge, row_heat, col_heat, turn = call(
        slab_edges_kernel,
        [shaped(THICK + 2, WIDE), shaped(THICK + 1, WIDE), thick, thick, thick],
        scratch=((THICK, WIDE),),
        cost=64,
    )(wide, to_far(s_deep))

    power, p_core, p_tile, loss, s_loss = call(
        power_kernel,
        [shaped(HALF, ROWS), shaped(HALF, RIM), shaped(HALF, RIM), shaped(OWN, ROWS), shaped(OWN, ROWS)],
        scratch=((HALF + 2, EXT),),
        cost=10,
    )(total, v0, v1, w2, diag, row_edge, col_edge, vert, ground, g_basis)
    p_far = to_far(power)
    q_tile = to_tile(p_tile)
    q_tile_far = to_tile(p_tile, 1)
    q_core_far = to_core_far(p_core)
    q_core = to_core(p_core)
    voltage_loss = unpack(loss, to_core(s_loss))

    out, s_out, final, s_final = call(
        sweeps_kernel,
        [shaped(DEEP, ROWS), shaped(DEEP, ROWS), shaped(LAYERS, ROWS), shaped(HALF, ROWS)],
        scratch=((LAYERS, WIDE), (THICK, WIDE), (THICK + 2, WIDE), (THICK + 2, WIDE)),
        scalars=2,
        cost=128,
    )(split, weights, power, p_far, q_core, q_core_far, q_tile, q_tile_far, warm, deep_edge, row_heat, col_heat, turn)
    g_final = to_far(s_final)
    final_warmth = unpack(out, to_core(s_out))
    mine, s_mine = call(update_kernel, [shaped(OWN, ROWS)] * 2, cost=4)(final, g_final, a6)
    updated_admittance = unpack(mine, to_core(s_mine))
    return voltage_loss, final_warmth, updated_admittance


def solution(mesh):
    spread = P("therm", "tile", None)
    return jax.shard_map(
        per_device,
        mesh=mesh,
        in_specs=(spread, spread, spread, spread, P(), spread, spread, P(), P()),
        out_specs=(spread, spread, spread),
        check_vma=False,
    )
```

```python
import functools

import jax
import jax.numpy as jnp
from jax import lax
from jax.experimental import pallas as pl
from jax.experimental.pallas import tpu as pltpu
from jax.sharding import PartitionSpec as P


LAYERS = 12
HALF = LAYERS // 2
OWN = 3
DEPTHS = 64
SLAB = DEPTHS // 2
DEEP = 16
ROWS = 16
RIM = 3
EXT = ROWS + 2 * RIM
HEATED = 7
SWEEPS = 4
WIDE = ROWS + 2 * SWEEPS
THICK = SLAB + SWEEPS
SCALE = 1.0 / 16.0
TINY = 1e-30

shunt_level = 0.05
pad_conductance = 4.0
via_conductance = 2.0
thermal_slope = 0.2
sink_level = 0.1

F32 = jnp.float32


def place():
    therm = lax.axis_index("therm")
    return therm // 2, therm % 2


def shaped(*dims):
    return jax.ShapeDtypeStruct(dims + (8, 128), F32)


def call(kernel, outs, scratch=(), scalars=0, cost=0, raw_in=False, raw_out=False, room=4):
    def held(out):
        return out if raw_out else pltpu.VMEM(out.shape, out.dtype)

    def run(*args):
        smem = [pl.BlockSpec(memory_space=pltpu.SMEM)] * scalars
        fields = args[scalars:]
        space = pltpu.HBM if raw_in else pltpu.VMEM
        fields = [pltpu.with_memory_space_constraint(v, space) for v in fields]
        own = [pltpu.VMEM(v.shape, v.dtype) for v in fields] if raw_in else []
        own += [pltpu.SemaphoreType.DMA((4,))] if raw_in else []
        return pl.pallas_call(
            kernel,
            out_shape=jax.tree.map(held, outs),
            in_specs=smem + [pl.BlockSpec(memory_space=space)] * len(fields),
            out_specs=jax.tree.map(lambda _: pl.BlockSpec(memory_space=pltpu.VMEM), outs),
            scratch_shapes=[pltpu.VMEM(dims + (8, 128), F32) for dims in scratch] + own,
            compiler_params=pltpu.CompilerParams(vmem_limit_bytes=room * 1024 * 1024),
            cost_estimate=pl.CostEstimate(flops=0, bytes_accessed=int(cost * 3.4e6), transcendentals=0),
        )(*args[:scalars], *fields)

    return run


def raw_view(value):
    n, rows, width = value.shape
    split = value.reshape(n, rows // 8, 8, width // 128, 128).transpose(0, 1, 3, 2, 4)
    return split.reshape(n, rows // 8, 8 * (width // 128), 128)


def raw_back(value):
    n, blocks, high, lanes = value.shape
    split = value.reshape(n, blocks, high // 8, 8, lanes).transpose(0, 1, 3, 2, 4)
    return split.reshape(n, blocks * 8, (high // 8) * lanes)


def at_row(ref, n, chunk, row):
    return ref[n, chunk * 2 + row // 8, pl.ds(row % 8, 8, stride=8), :]


def loop(count, body):
    def step(i, carry):
        body(i)
        return carry

    lax.fori_loop(0, count, step, 0)


def iotas():
    return lax.broadcasted_iota(jnp.int32, (8, 128), 0), lax.broadcasted_iota(jnp.int32, (8, 128), 1)


def after(v, lane):
    r = pltpu.roll(v, 127, 1)
    return jnp.where(lane == 127, pltpu.roll(r, 7, 0), r)


def before(v, lane):
    r = pltpu.roll(v, 1, 1)
    return jnp.where(lane == 0, pltpu.roll(r, 1, 0), r)


def inverse(v):
    r = pl.reciprocal(v, approx=True)
    r = r * (2.0 - v * r)
    return r * (2.0 - v * r)


def harmonic(a, b):
    return a * b * inverse(jnp.maximum(a + b, TINY))


def pack_kernel(value, own, send, held, sems):
    _, core = place()
    parts = sems.shape[0]
    size = value.shape[0] // parts
    copies = [
        pltpu.make_async_copy(value.at[pl.ds(p * size, size)], held.at[pl.ds(p * size, size)], sems.at[p])
        for p in range(parts)
    ]
    for copy in copies:
        copy.start()
    for p, copy in enumerate(copies):
        copy.wait()

        def body(i, p=p):
            n = p * size + i
            for row in range(ROWS):
                own[n, row] = at_row(held, n, core, row)
                send[n, row] = at_row(held, n, 1 - core, row)

        loop(size, body)


def pack_args_kernel(classes, sink, category, link, contact, own, send, *held_sems):
    _, core = place()
    held, sems = held_sems[:4], held_sems[4]
    copies = [
        pltpu.make_async_copy(ref, to, sems.at[p])
        for p, (ref, to) in enumerate(zip((sink, category, link, contact), held))
    ]
    for copy in copies:
        copy.start()
    for copy in copies:
        copy.wait()
    sink, category, link, contact = held

    def body(n):
        for row in range(ROWS):
            for chunk, out in ((core, own), (1 - core, send)):
                kind = at_row(category, n, chunk, row)
                table = jnp.full((8, 128), classes[0], F32)
                for number in range(1, 8):
                    table = jnp.where(kind == number, classes[number], table)
                out[n, row] = at_row(sink, n, chunk, row)
                out[OWN + n, row] = table * SCALE
                out[2 * OWN + n, row] = at_row(link, n, chunk, row).astype(F32) * (via_conductance * SCALE)
                out[3 * OWN + n, row] = at_row(contact, n, chunk, row).astype(F32) * (
                    pad_conductance * SCALE
                ) + (shunt_level * SCALE)

    loop(OWN, body)


def weigh(weights, parts, acc):
    def rows(block):
        total = [jnp.zeros((8, 128), F32)] * (4 * LAYERS)
        for ref, first, base in parts:

            def step(z, total):
                field = [ref[first + z, block * 4 + k] for k in range(4)]
                out = []
                for layer in range(LAYERS):
                    w = weights[layer, base + z]
                    out += [total[layer * 4 + k] + w * field[k] for k in range(4)]
                return tuple(out)

            total = lax.fori_loop(0, DEEP, step, tuple(total), unroll=4)
        for layer in range(LAYERS):
            for k in range(4):
                acc[layer, block * 4 + k] = total[layer * 4 + k]

    loop(ROWS // 4, rows)


def heat_kernel(weights, t_own, t_got, part):
    far, core = place()
    weigh(
        weights,
        ((t_own, 0, SLAB * far + DEEP * core), (t_got, 0, SLAB * far + DEEP * (1 - core))),
        part,
    )


def merge_kernel(part, a_own, a_got, a6, s_far, s_core_far, s_tile_far, s_core, s_tile):
    far, core = place()

    def merge(n):
        for row in range(ROWS):
            for ch in range(4):
                a6[ch, OWN * core + n, row] = a_own[ch * OWN + n, row]
                a6[ch, OWN * (1 - core) + n, row] = a_got[ch * OWN + n, row]

    loop(OWN, merge)
    to_core, to_tile = (ROWS - RIM) * (1 - core), (ROWS - RIM) * core

    def heats(n):
        for row in range(ROWS):
            s_far[n, row] = part[5 * (1 - far) + n, row]
        for k in range(RIM):
            s_core_far[n, k] = part[5 * (1 - far) + n, to_core + k]
            s_tile_far[n, k] = part[5 * (1 - far) + n, to_tile + k]
            s_core[n, k] = part[5 * far + n, to_core + k]
            s_tile[n, k] = part[5 * far + n, to_tile + k]

    loop(HEATED, heats)
    edge = 5 * (1 - far)
    for n, ch in ((HEATED, 0), (HEATED + 1, 2)):
        for row in range(ROWS):
            s_far[n, row] = a6[ch, edge, row]
        for k in range(RIM):
            s_core_far[n, k] = a6[ch, edge, to_core + k]
            s_tile_far[n, k] = a6[ch, edge, to_tile + k]

    def args(o):
        for ch in range(4):
            for k in range(RIM):
                s_core[HEATED + ch * HALF + o, k] = a6[ch, o, to_core + k]
                s_tile[HEATED + ch * HALF + o, k] = a6[ch, o, to_tile + k]

    loop(HALF, args)


def apply(v, o, row, diag, row_edge, col_edge, vert, lane):
    here = v[o + 1, row]
    ce = col_edge[o, row]
    return (
        diag[o, row] * here
        - row_edge[o, row - 1] * v[o + 1, row - 1]
        - row_edge[o, row] * v[o + 1, row + 1]
        - ce * after(here, lane)
        - before(ce * here, lane)
        - vert[o + 1, row] * v[o + 2, row]
        - vert[o, row] * v[o, row]
    )


def basis_kernel(
    part, a6, g_far, g_core_far, g_tile_far, g_core, g_tile,
    v0, v1, v2, diag, row_edge, col_edge, vert, ground, s_basis, inv, lat,
):
    far, core = place()
    sub, lane = iotas()
    from_core, from_tile = (EXT - RIM) * (1 - core), (EXT - RIM) * core
    zero = jnp.zeros((8, 128), F32)

    def heats(n):
        def one(row, heat):
            inv[n, row] = inverse(1.0 + thermal_slope * heat)

        for k in range(ROWS):
            one(RIM + k, part[5 * far + n, k] + g_far[n, k])
        for k in range(RIM):
            one(from_core + k, g_core[n, k] + g_core_far[n, k])
            one(from_tile + k, g_tile[n, k] + g_tile_far[n, k])

    loop(HEATED, heats)
    lower = far.astype(F32)
    halo, none = 7 * (1 - far), 7 * far

    def rim(row, b, up):
        v0[halo, row] = b
        v0[none, row] = zero
        vert[0, row] = up * inv[0, row] * lower

    for k in range(ROWS):
        rim(RIM + k, g_far[HEATED, k], g_far[HEATED + 1, k])
    for k in range(RIM):
        rim(from_core + k, g_core_far[HEATED, k], g_core_far[HEATED + 1, k])
        rim(from_tile + k, g_tile_far[HEATED, k], g_tile_far[HEATED + 1, k])
    for row in range(EXT):
        for edge in (0, 7):
            v1[edge, row] = zero
            v2[edge, row] = zero

    def fields(o):
        def one(row, b, g, up, gr):
            warm = inv[o + far, row]
            v0[o + 1, row] = b
            lat[o, row] = g * warm
            vert[o + 1, row] = up * warm
            ground[o, row] = gr

        for k in range(ROWS):
            one(RIM + k, *[a6[ch, o, k] for ch in range(4)])
        for k in range(RIM):
            one(from_core + k, *[g_core[HEATED + ch * HALF + o, k] for ch in range(4)])
            one(from_tile + k, *[g_tile[HEATED + ch * HALF + o, k] for ch in range(4)])

    loop(HALF, fields)
    last = (sub == 7) & (lane == 127)

    def edges(o):
        for row in range(EXT - 1):
            row_edge[o, row] = harmonic(lat[o, row], lat[o, row + 1])
        for row in range(1, EXT - 1):
            here = lat[o, row]
            ce = jnp.where(last, 0.0, harmonic(here, after(here, lane)))
            col_edge[o, row] = ce
            diag[o, row] = (
                ground[o, row] + vert[o + 1, row] + vert[o, row]
                + row_edge[o, row - 1] + row_edge[o, row] + ce + before(ce, lane)
            )

    loop(HALF, edges)

    def first(o):
        for row in range(1, EXT - 1):
            v1[o + 1, row] = apply(v0, o, row, diag, row_edge, col_edge, vert, lane)

    loop(HALF, first)

    def second(o):
        for row in range(2, EXT - 2):
            v2[o + 1, row] = apply(v1, o, row, diag, row_edge, col_edge, vert, lane)

    loop(HALF, second)
    edge = 5 * (1 - far) + 1
    for k in range(EXT - 4):
        s_basis[0, k] = v1[edge, 2 + k]
        s_basis[1, k] = v2[edge, 2 + k]


def moments_kernel(v0, v1, v2, diag, row_edge, col_edge, vert, got, w2, out):
    far, _ = place()
    _, lane = iotas()

    def copy(n):
        for row in range(2, EXT - 2):
            w2[n, row] = v2[n, row]

    loop(HALF + 2, copy)
    edge, halo = 5 * (1 - far) + 1, 7 * (1 - far)
    for k in range(EXT - 4):
        row = 2 + k
        link = vert[6 * (1 - far), row]
        w2[edge, row] = v2[edge, row] - link * got[0, k]
        w2[halo, row] = got[1, k] - link * v1[edge, row]

    def body(o, sums):
        sums = list(sums)
        for row in range(RIM, RIM + ROWS):
            a, b, c = v0[o + 1, row], v1[o + 1, row], w2[o + 1, row]
            d = apply(w2, o, row, diag, row_edge, col_edge, vert, lane)
            for n, term in enumerate((a * a, a * b, b * b, b * c, c * c, c * d)):
                sums[n] = sums[n] + term
        return tuple(sums)

    sums = lax.fori_loop(0, HALF, body, (jnp.zeros((8, 128), F32),) * 6)
    for n in range(6):
        out[0, pl.ds(n, 1), :] = jnp.full((1, 128), jnp.sum(sums[n]), F32)
    out[0, pl.ds(6, 2), :] = jnp.zeros((2, 128), F32)
    out[1] = jnp.zeros((8, 128), F32)


def two_sum(a, b):
    s = a + b
    t = s - a
    return s, (a - (s - t)) + (b - t)


def two_prod(a, b):
    def split(v):
        t = v * 4097.0
        high = t - (t - v)
        return high, v - high

    p = a * b
    (ah, al), (bh, bl) = split(a), split(b)
    return p, ((ah * bh - p) + ah * bl + al * bh) + al * bl


def pair_add(a, b):
    s, e = two_sum(a[0], b[0])
    e = e + (a[1] + b[1])
    high = s + e
    return high, e - (high - s)


def pair_mul(a, b):
    p, e = two_prod(a[0], b[0])
    e = e + (a[0] * b[1] + a[1] * b[0])
    high = p + e
    return high, e - (high - p)


def pair_neg(a):
    return -a[0], -a[1]


def pair_div(a, b):
    q = a[0] / b[0]
    r = pair_add(a, pair_neg(pair_mul(b, (q, jnp.zeros_like(q)))))
    q2 = (r[0] + r[1]) / b[0]
    high = q + q2
    return high, q2 - (high - q)


def coefficients(m):
    mean, m2, m3, m4, m5 = [pair_div(v, m[0]) for v in m[1:]]
    low = pair_neg(mean)

    def lowered(seq):
        return [pair_add(b, pair_mul(low, a)) for a, b in zip(seq, seq[1:])]

    one = (jnp.ones_like(mean[0]), jnp.zeros_like(mean[0]))
    seq = [one, mean, m2, m3, m4, m5]
    seq = lowered(seq)
    central = []
    for power in range(2, 6):
        seq = lowered(seq)
        central.append(seq[0])
    c2, c3, c4, c5 = [v[0] + v[1] for v in central]
    s = mean[0] + mean[1]
    ok1 = c2 > 3e-8 * s * s
    c2 = jnp.where(ok1, c2, 1.0)
    skew = c3 / c2
    n2 = c4 - skew * c3 - c2 * c2
    ok2 = ok1 & (n2 > 1e-6 * c2 * c2) & (n2 > 3e-8 * (s * s) * (s * s))
    n2 = jnp.where(ok2, n2, 1.0)
    tq = c5 - 2.0 * skew * c4 + (skew * skew - 2.0 * c2) * c3 + 2.0 * skew * c2 * c2
    a2 = s + tq / n2
    a1 = s + skew
    b1, b2 = c2, n2 / c2
    d0 = s
    d1 = a1 - b1 / d0
    d2 = a2 - b2 / d1
    y0 = 1.0 / d0
    y1 = jnp.where(ok1, -y0 / d1, 0.0)
    y2 = jnp.where(ok2, -y1 / d2, 0.0)
    z2 = y2
    z1 = y1 - jnp.where(ok2, b2 * z2 / d1, 0.0)
    z0 = y0 - jnp.where(ok1, b1 * z1 / d0, 0.0)
    k2 = z2
    k1 = z1 - z2 * (skew + 2.0 * s)
    k0 = z0 - z1 * s + z2 * (s * s + skew * s - c2)
    return k0 * SCALE, k1 * SCALE, k2 * SCALE


def power_kernel(
    total, v0, v1, w2, diag, row_edge, col_edge, vert, ground, got,
    power, s_core, s_tile, loss, s_loss, volts,
):
    far, core = place()
    _, lane = iotas()
    spread = [
        (
            jnp.broadcast_to(total[0, pl.ds(n, 1), :], (8, 128)),
            jnp.broadcast_to(total[1, pl.ds(n, 1), :], (8, 128)),
        )
        for n in range(6)
    ]
    c0, c1, c2 = coefficients(spread)
    halo = 7 * (1 - far)

    def combine(n):
        for row in range(2, EXT - 2):
            volts[n, row] = c0 * v0[n, row] + c1 * v1[n, row] + c2 * w2[n, row]

    loop(HALF + 2, combine)
    for k in range(EXT - 4):
        row = 2 + k
        volts[halo, row] = c0 * v0[halo, row] + c1 * got[0, k] + c2 * w2[halo, row]

    def body(o):
        for k in range(ROWS):
            row = RIM + k
            x = volts[o + 1, row]
            near = after(x, lane) - x
            q = col_edge[o, row] * near * near
            q = q + before(q, lane)
            for edge, other in (
                (row_edge[o, row - 1], volts[o + 1, row - 1]),
                (row_edge[o, row], volts[o + 1, row + 1]),
                (vert[o + 1, row], volts[o + 2, row]),
                (vert[o, row], volts[o, row]),
            ):
                d = x - other
                q = q + edge * d * d
            power[o, k] = 16.0 * ground[o, row] * x * x + 8.0 * q

    loop(HALF, body)
    to_core, to_tile = (ROWS - RIM) * (1 - core), (ROWS - RIM) * core

    def sides(o):
        for k in range(RIM):
            s_core[o, k] = power[o, to_core + k]
            s_tile[o, k] = power[o, to_tile + k]

    loop(HALF, sides)

    def outs(n):
        for k in range(ROWS):
            loss[n, k] = volts[1 + OWN * core + n, RIM + k]
            s_loss[n, k] = volts[1 + OWN * (1 - core) + n, RIM + k]

    loop(OWN, outs)


def slab_rim_kernel(t_own, t_got, k_own, k_got, s_core, s_tile):
    _, core = place()
    to_core, to_tile = (ROWS - SWEEPS) * (1 - core), (ROWS - SWEEPS) * core

    def body(n):
        for f, (own, got) in enumerate(((t_own, t_got), (k_own, k_got))):
            for ref, z in ((own, DEEP * core + n), (got, DEEP * (1 - core) + n)):
                for k in range(SWEEPS):
                    s_core[f, z, k] = ref[n, to_core + k]
                    s_tile[f, z, k] = ref[n, to_tile + k]

    loop(DEEP, body)


def slab_wide_kernel(t_own, t_got, k_own, k_got, g_core, g_tile, wide, s_far):
    far, core = place()
    from_core, from_tile = (WIDE - SWEEPS) * (1 - core), (WIDE - SWEEPS) * core

    def body(n):
        for f, (own, got) in enumerate(((t_own, t_got), (k_own, k_got))):
            for ref, z in ((own, DEEP * core + n), (got, DEEP * (1 - core) + n)):
                for k in range(ROWS):
                    wide[f, z, SWEEPS + k] = ref[n, k]
                for k in range(SWEEPS):
                    wide[f, z, from_core + k] = g_core[f, z, k]
                    wide[f, z, from_tile + k] = g_tile[f, z, k]

    loop(DEEP, body)
    first = (SLAB - SWEEPS) * (1 - far)

    def send(n):
        for f in range(2):
            for row in range(WIDE):
                s_far[f, n, row] = wide[f, first + n, row]

    loop(SWEEPS, send)


def slab_edges_kernel(wide, g_far, warm, deep_edge, row_edge, col_edge, turn, cond):
    far, _ = place()
    sub, lane = iotas()
    zero = jnp.zeros((8, 128), F32)

    def body(n):
        for row in range(WIDE):
            warm[1 + SWEEPS * far + n, row] = wide[0, n, row]
            cond[SWEEPS * far + n, row] = wide[1, n, row]

    loop(SLAB, body)

    def rim(n):
        for row in range(WIDE):
            warm[1 + SLAB * (1 - far) + n, row] = g_far[0, n, row]
            cond[SLAB * (1 - far) + n, row] = g_far[1, n, row]

    loop(SWEEPS, rim)
    for row in range(WIDE):
        for n in (0, THICK + 1):
            warm[n, row] = zero
        for n in (0, THICK):
            deep_edge[n, row] = zero

    def deep(n):
        for row in range(WIDE):
            deep_edge[n + 1, row] = harmonic(cond[n, row], cond[n + 1, row])

    loop(THICK - 1, deep)
    last = (sub == 7) & (lane == 127)

    def edges(n):
        for row in range(WIDE - 1):
            row_edge[n, row] = harmonic(cond[n, row], cond[n, row + 1])
        for row in range(1, WIDE - 1):
            here = cond[n, row]
            ce = jnp.where(last, 0.0, harmonic(here, after(here, lane)))
            col_edge[n, row] = ce
            turn[n, row] = inverse(
                sink_level + deep_edge[n, row] + deep_edge[n + 1, row]
                + row_edge[n, row - 1] + row_edge[n, row] + ce + before(ce, lane)
            )

    loop(THICK, edges)


def sweeps_kernel(
    split, weights, power, p_far, p_core, p_core_far, p_tile, p_tile_far,
    warm, deep_edge, row_edge, col_edge, turn,
    out, s_out, final, s_final,
    joule, source, one, two,
):
    far, core = place()
    _, lane = iotas()
    zero = jnp.zeros((8, 128), F32)
    from_core = 1 + (EXT - RIM) * (1 - core)
    from_tile = 1 + (EXT - RIM) * core

    def gather(o):
        for layer, mid, by_core, by_tile in (
            (HALF * far + o, power, p_core, p_tile),
            (HALF * (1 - far) + o, p_far, p_core_far, p_tile_far),
        ):
            for k in range(ROWS):
                joule[layer, SWEEPS + k] = mid[o, k]
            for k in range(RIM):
                joule[layer, from_core + k] = by_core[o, k]
                joule[layer, from_tile + k] = by_tile[o, k]
            joule[layer, 0] = zero
            joule[layer, WIDE - 1] = zero

    loop(HALF, gather)
    base = (SLAB - SWEEPS) * far

    def sources(block):
        field = [[joule[layer, block * 4 + k] for k in range(4)] for layer in range(LAYERS)]

        def depth(n, carry):
            total = [zero] * 4
            for layer in range(LAYERS):
                w = split[layer, base + n]
                total = [total[k] + w * field[layer][k] for k in range(4)]
            for k in range(4):
                source[n, block * 4 + k] = total[k]
            return carry

        lax.fori_loop(0, THICK, depth, 0)

    loop(WIDE // 4, sources)
    for ref in (one, two):
        for row in range(WIDE):
            ref[0, row] = zero
            ref[THICK + 1, row] = zero

    before_ref = warm
    for sweep in range(1, SWEEPS + 1):
        after_ref = one if sweep % 2 else two
        start = sweep * far

        def step(i, src=before_ref, dst=after_ref, sweep=sweep, start=start):
            n = start + i
            for row in range(sweep, WIDE - sweep):
                here = src[n + 1, row]
                ce = col_edge[n, row]
                flow = source[n, row] + ce * after(here, lane) + before(ce * here, lane)
                flow = flow + row_edge[n, row - 1] * src[n + 1, row - 1] + row_edge[n, row] * src[n + 1, row + 1]
                flow = flow + deep_edge[n, row] * src[n, row] + deep_edge[n + 1, row] * src[n + 2, row]
                dst[n + 1, row] = flow * turn[n, row]

        loop(THICK - sweep, step)
        before_ref = after_ref

    def outs(n):
        for k in range(ROWS):
            out[n, k] = before_ref[1 + SWEEPS * far + DEEP * core + n, SWEEPS + k]
            s_out[n, k] = before_ref[1 + SWEEPS * far + DEEP * (1 - core) + n, SWEEPS + k]

    loop(DEEP, outs)
    weigh(
        weights,
        ((out, 0, SLAB * far + DEEP * core), (s_out, 0, SLAB * far + DEEP * (1 - core))),
        final,
    )

    def sends(o):
        for k in range(ROWS):
            s_final[o, k] = final[HALF * (1 - far) + o, k]

    loop(HALF, sends)


def update_kernel(final, got, a6, mine, send):
    far, core = place()

    def body(n):
        for half, out in ((core, mine), (1 - core, send)):
            o = OWN * half + n
            for k in range(ROWS):
                heat = final[HALF * far + o, k] + got[o, k]
                out[n, k] = (16.0 * a6[1, o, k]) * inverse(1.0 + thermal_slope * heat)

    loop(OWN, body)


def unpack_kernel(own, got, out):
    _, core = place()

    def body(n):
        for k in range(ROWS):
            out[n, core * 2 + k // 8, pl.ds(k % 8, 8, stride=8), :] = own[n, k]
            out[n, (1 - core) * 2 + k // 8, pl.ds(k % 8, 8, stride=8), :] = got[n, k]

    loop(own.shape[0], body)


def unpack(own, got):
    n = own.shape[0]
    out = jax.ShapeDtypeStruct((n, 4, 64, 128), F32)
    return raw_back(call(unpack_kernel, out, cost=n / 10, raw_out=True)(own, got))


def pack(value):
    n = value.shape[0]
    return call(pack_kernel, [shaped(n, ROWS)] * 2, cost=2, raw_in=True)(raw_view(value))


def to_core(value):
    return lax.ppermute(value, "therm", [(i, i ^ 1) for i in range(4)])


def to_far(value):
    return lax.ppermute(value, "therm", [(i, i ^ 2) for i in range(4)])


def to_core_far(value):
    return lax.ppermute(value, "therm", [(i, i ^ 3) for i in range(4)])


def to_tile(value, cross=0):
    pairs = []
    for t in range(lax.axis_size("tile") - 1):
        for half in range(2):
            low = 4 * t + 2 * half + 1
            high = 4 * (t + 1) + 2 * (half ^ cross)
            pairs += [(low, high), (high, low)]
    return lax.ppermute(value, ("tile", "therm"), pairs)


def add_pairs(a, b):
    high, low = pair_add((a[0], a[1]), (b[0], b[1]))
    return jnp.stack([high, low])


def along_core_and_x(values):
    values = add_pairs(values, to_core(values))
    peers = []
    for bits in (2, 3, 1):
        pairs = [
            (4 * t + h, 4 * (t ^ (bits & 1)) + (h ^ (bits & 2)))
            for t in range(lax.axis_size("tile"))
            for h in range(4)
        ]
        peers.append(lax.ppermute(values, ("tile", "therm"), pairs))
    for peer in peers:
        values = add_pairs(values, peer)
    return values


def along_tile(values, unit):
    peers = [
        lax.ppermute(values, "tile", [(t, t ^ (unit * k)) for t in range(lax.axis_size("tile"))])
        for k in (2, 1, 3)
    ]
    for peer in peers:
        values = add_pairs(values, peer)
    return values


def tied(value, to):
    return lax.optimization_barrier((value, to))[0]


def per_device(
    sink_current,
    metal_category,
    upward_link_flag,
    supply_contact_flag,
    baseline_admittance,
    beginning_warmth,
    cell_diffusivity,
    dissipation_split,
    probe_weighting,
):
    weights, split = probe_weighting, dissipation_split.T
    t_own, t_send = pack(beginning_warmth)
    t_got = to_core(t_send)
    a_own, a_send = call(pack_args_kernel, [shaped(4 * OWN, ROWS)] * 2, scalars=1, cost=3, raw_in=True)(
        baseline_admittance,
        *[raw_view(v) for v in (sink_current, metal_category, upward_link_flag, supply_contact_flag)],
    )
    a_got = to_core(a_send)
    part = call(heat_kernel, shaped(LAYERS, ROWS), scalars=1, cost=3, room=2)(weights, t_own, t_got)
    a6, s_far, s_core_far, s_tile_far, s_core, s_tile = call(
        merge_kernel,
        [
            shaped(4, HALF, ROWS),
            shaped(HEATED + 2, ROWS),
            shaped(HEATED + 2, RIM),
            shaped(HEATED + 2, RIM),
            shaped(HEATED + 4 * HALF, RIM),
            shaped(HEATED + 4 * HALF, RIM),
        ],
        cost=1.5,
        room=2,
    )(part, a_own, a_got)
    g_far = to_far(s_far)
    g_tile = to_tile(s_tile)
    g_tile_far = to_tile(s_tile_far, 1)
    g_core_far = to_core_far(s_core_far)
    g_core = to_core(s_core)

    k_own, k_send = pack(tied(cell_diffusivity, s_far))

    field = shaped(HALF + 2, EXT)
    coef = shaped(HALF, EXT)
    v0, v1, v2, diag, row_edge, col_edge, vert, ground, s_basis = call(
        basis_kernel,
        [field, field, field, coef, coef, coef, shaped(HALF + 1, EXT), coef, shaped(2, EXT - 4)],
        scratch=((HEATED, EXT), (HALF, EXT)),
        cost=3,
    )(part, a6, g_far, g_core_far, g_tile_far, g_core, g_tile)
    g_basis = to_far(s_basis)
    k_got = to_core(tied(k_send, s_basis))
    rim = shaped(2, SLAB, SWEEPS)
    k_core, k_tile = call(slab_rim_kernel, [rim, rim], cost=0.4)(t_own, t_got, k_own, k_got)
    wide, s_deep = call(slab_wide_kernel, [shaped(2, SLAB, WIDE), shaped(2, SWEEPS, WIDE)], cost=0.6)(
        t_own, t_got, k_own, k_got, to_core(k_core), to_tile(k_tile)
    )
    w2, sums = call(moments_kernel, [field, shaped(2)], cost=0.9)(
        tied(v0, k_tile), v1, v2, diag, row_edge, col_edge, vert, g_basis
    )
    values = along_core_and_x(sums)
    values, s_deep = lax.optimization_barrier((values, s_deep))
    values = along_tile(values, 2)
    total = along_tile(values, 8)
    thick = shaped(THICK, WIDE)
    warm, deep_edge, row_heat, col_heat, turn = call(
        slab_edges_kernel,
        [shaped(THICK + 2, WIDE), shaped(THICK + 1, WIDE), thick, thick, thick],
        scratch=((THICK, WIDE),),
        cost=9.5,
        room=5,
    )(wide, to_far(s_deep))

    power, p_core, p_tile, loss, s_loss = call(
        power_kernel,
        [shaped(HALF, ROWS), shaped(HALF, RIM), shaped(HALF, RIM), shaped(OWN, ROWS), shaped(OWN, ROWS)],
        scratch=((HALF + 2, EXT),),
        cost=1.4,
    )(total, v0, v1, w2, diag, row_edge, col_edge, vert, ground, g_basis)
    p_far = to_far(power)
    q_tile = to_tile(p_tile)
    q_tile_far = to_tile(p_tile, 1)
    q_core_far = to_core_far(p_core)
    q_core = to_core(p_core)
    voltage_loss = unpack(loss, to_core(s_loss))

    out, s_out, final, s_final = call(
        sweeps_kernel,
        [shaped(DEEP, ROWS), shaped(DEEP, ROWS), shaped(LAYERS, ROWS), shaped(HALF, ROWS)],
        scratch=((LAYERS, WIDE), (THICK, WIDE), (THICK + 2, WIDE), (THICK + 2, WIDE)),
        scalars=2,
        cost=25,
        room=14,
    )(split, weights, power, p_far, q_core, q_core_far, q_tile, q_tile_far, warm, deep_edge, row_heat, col_heat, turn)
    g_final = to_far(s_final)
    final_warmth = unpack(out, to_core(s_out))
    g_final = tied(g_final, final_warmth)
    mine, s_mine = call(update_kernel, [shaped(OWN, ROWS)] * 2, cost=0.4)(final, g_final, a6)
    updated_admittance = unpack(mine, to_core(s_mine))
    return voltage_loss, final_warmth, updated_admittance


def solution(mesh):
    spread = P("therm", "tile", None)
    return jax.shard_map(
        per_device,
        mesh=mesh,
        in_specs=(spread, spread, spread, spread, P(), spread, spread, P(), P()),
        out_specs=(spread, spread, spread),
        check_vma=False,
    )
```

```python
import functools

import jax
import jax.numpy as jnp
from jax import lax
from jax.experimental import pallas as pl
from jax.experimental.pallas import tpu as pltpu
from jax.sharding import PartitionSpec as P


LAYERS = 12
HALF = LAYERS // 2
OWN = 3
DEPTHS = 64
SLAB = DEPTHS // 2
DEEP = 16
ROWS = 16
RIM = 3
EXT = ROWS + 2 * RIM
HEATED = 7
SWEEPS = 4
WIDE = ROWS + 2 * SWEEPS
THICK = SLAB + SWEEPS
SCALE = 1.0 / 16.0
TINY = 1e-30

shunt_level = 0.05
pad_conductance = 4.0
via_conductance = 2.0
thermal_slope = 0.2
sink_level = 0.1

F32 = jnp.float32


def place():
    therm = lax.axis_index("therm")
    return therm // 2, therm % 2


def shaped(*dims):
    return jax.ShapeDtypeStruct(dims + (8, 128), F32)


def call(kernel, outs, scratch=(), scalars=0, cost=0, raw_in=False, raw_out=False, room=4, alias={}):
    def held(out):
        return out if raw_out else pltpu.VMEM(out.shape, out.dtype)

    def run(*args):
        smem = [pl.BlockSpec(memory_space=pltpu.SMEM)] * scalars
        fields = args[scalars:]
        space = pltpu.HBM if raw_in else pltpu.VMEM
        fields = [pltpu.with_memory_space_constraint(v, space) for v in fields]
        own = [pltpu.VMEM(v.shape, v.dtype) for v in fields] if raw_in else []
        own += [pltpu.SemaphoreType.DMA((4,))] if raw_in else []
        return pl.pallas_call(
            kernel,
            out_shape=jax.tree.map(held, outs),
            in_specs=smem + [pl.BlockSpec(memory_space=space)] * len(fields),
            input_output_aliases=alias,
            out_specs=jax.tree.map(lambda _: pl.BlockSpec(memory_space=pltpu.VMEM), outs),
            scratch_shapes=[pltpu.VMEM(dims + (8, 128), F32) for dims in scratch] + own,
            compiler_params=pltpu.CompilerParams(vmem_limit_bytes=room * 1024 * 1024),
            cost_estimate=pl.CostEstimate(flops=0, bytes_accessed=int(cost * 3.4e6), transcendentals=0),
        )(*args[:scalars], *fields)

    return run


def raw_view(value):
    n, rows, width = value.shape
    split = value.reshape(n, rows // 8, 8, width // 128, 128).transpose(0, 1, 3, 2, 4)
    return split.reshape(n, rows // 8, 8 * (width // 128), 128)


def raw_back(value):
    n, blocks, high, lanes = value.shape
    split = value.reshape(n, blocks, high // 8, 8, lanes).transpose(0, 1, 3, 2, 4)
    return split.reshape(n, blocks * 8, (high // 8) * lanes)


def at_row(ref, n, chunk, row):
    return ref[n, chunk * 2 + row // 8, pl.ds(row % 8, 8, stride=8), :]


def loop(count, body, unroll=4):
    def step(i, carry):
        body(i)
        return carry

    lax.fori_loop(0, count, step, 0, unroll=min(unroll, count))


def iotas():
    return lax.broadcasted_iota(jnp.int32, (8, 128), 0), lax.broadcasted_iota(jnp.int32, (8, 128), 1)


def after(v, lane):
    r = pltpu.roll(v, 127, 1)
    return jnp.where(lane == 127, pltpu.roll(r, 7, 0), r)


def before(v, lane):
    r = pltpu.roll(v, 1, 1)
    return jnp.where(lane == 0, pltpu.roll(r, 1, 0), r)


def inverse(v):
    r = pl.reciprocal(v, approx=True)
    r = r * (2.0 - v * r)
    return r * (2.0 - v * r)


def harmonic(a, b):
    return a * b * inverse(jnp.maximum(a + b, TINY))


def pack_kernel(value, own, send, held, sems):
    _, core = place()
    parts = sems.shape[0]
    size = value.shape[0] // parts
    copies = [
        pltpu.make_async_copy(value.at[pl.ds(p * size, size)], held.at[pl.ds(p * size, size)], sems.at[p])
        for p in range(parts)
    ]
    for copy in copies:
        copy.start()
    for p, copy in enumerate(copies):
        copy.wait()

        def body(i, p=p):
            n = p * size + i
            for row in range(ROWS):
                own[n, row] = at_row(held, n, core, row)
                send[n, row] = at_row(held, n, 1 - core, row)

        loop(size, body)


def pack_args_kernel(classes, sink, category, link, contact, own, send, *held_sems):
    _, core = place()
    held, sems = held_sems[:4], held_sems[4]
    copies = [
        pltpu.make_async_copy(ref, to, sems.at[p])
        for p, (ref, to) in enumerate(zip((sink, category, link, contact), held))
    ]
    for copy in copies:
        copy.start()
    for copy in copies:
        copy.wait()
    sink, category, link, contact = held

    def body(n):
        for row in range(ROWS):
            for chunk, out in ((core, own), (1 - core, send)):
                kind = at_row(category, n, chunk, row)
                table = jnp.full((8, 128), classes[0], F32)
                for number in range(1, 8):
                    table = jnp.where(kind == number, classes[number], table)
                out[n, row] = at_row(sink, n, chunk, row)
                out[OWN + n, row] = table * SCALE
                out[2 * OWN + n, row] = at_row(link, n, chunk, row).astype(F32) * (via_conductance * SCALE)
                out[3 * OWN + n, row] = at_row(contact, n, chunk, row).astype(F32) * (
                    pad_conductance * SCALE
                ) + (shunt_level * SCALE)

    loop(OWN, body)


def weigh(weights, parts, acc):
    def rows(block):
        total = [jnp.zeros((8, 128), F32)] * (4 * LAYERS)
        for ref, first, base in parts:

            def step(z, total):
                field = [ref[first + z, block * 4 + k] for k in range(4)]
                out = []
                for layer in range(LAYERS):
                    w = weights[layer, base + z]
                    out += [total[layer * 4 + k] + w * field[k] for k in range(4)]
                return tuple(out)

            total = lax.fori_loop(0, DEEP, step, tuple(total), unroll=16)
        for layer in range(LAYERS):
            for k in range(4):
                acc[layer, block * 4 + k] = total[layer * 4 + k]

    loop(ROWS // 4, rows)


def heat_kernel(weights, t_own, t_got, part):
    far, core = place()
    weigh(
        weights,
        ((t_own, 0, SLAB * far + DEEP * core), (t_got, 0, SLAB * far + DEEP * (1 - core))),
        part,
    )


def merge_kernel(part, a_own, a_got, a6, s_far, s_core_far, s_tile_far, s_core, s_tile):
    far, core = place()

    def merge(n):
        for row in range(ROWS):
            for ch in range(4):
                a6[ch, OWN * core + n, row] = a_own[ch * OWN + n, row]
                a6[ch, OWN * (1 - core) + n, row] = a_got[ch * OWN + n, row]

    loop(OWN, merge)
    to_core, to_tile = (ROWS - RIM) * (1 - core), (ROWS - RIM) * core

    def heats(n):
        for row in range(ROWS):
            s_far[n, row] = part[5 * (1 - far) + n, row]
        for k in range(RIM):
            s_core_far[n, k] = part[5 * (1 - far) + n, to_core + k]
            s_tile_far[n, k] = part[5 * (1 - far) + n, to_tile + k]
            s_core[n, k] = part[5 * far + n, to_core + k]
            s_tile[n, k] = part[5 * far + n, to_tile + k]

    loop(HEATED, heats)
    edge = 5 * (1 - far)
    for n, ch in ((HEATED, 0), (HEATED + 1, 2)):
        for row in range(ROWS):
            s_far[n, row] = a6[ch, edge, row]
        for k in range(RIM):
            s_core_far[n, k] = a6[ch, edge, to_core + k]
            s_tile_far[n, k] = a6[ch, edge, to_tile + k]

    def args(o):
        for ch in range(4):
            for k in range(RIM):
                s_core[HEATED + ch * HALF + o, k] = a6[ch, o, to_core + k]
                s_tile[HEATED + ch * HALF + o, k] = a6[ch, o, to_tile + k]

    loop(HALF, args)


def apply(v, o, row, diag, row_edge, col_edge, vert, lane):
    here = v[o + 1, row]
    ce = col_edge[o, row]
    return (
        diag[o, row] * here
        - row_edge[o, row - 1] * v[o + 1, row - 1]
        - row_edge[o, row] * v[o + 1, row + 1]
        - ce * after(here, lane)
        - before(ce * here, lane)
        - vert[o + 1, row] * v[o + 2, row]
        - vert[o, row] * v[o, row]
    )


def basis_kernel(
    part, a6, g_far, g_core_far, g_tile_far, g_core, g_tile,
    v0, v1, v2, diag, row_edge, col_edge, vert, ground, s_basis, inv, lat,
):
    far, core = place()
    sub, lane = iotas()
    from_core, from_tile = (EXT - RIM) * (1 - core), (EXT - RIM) * core
    zero = jnp.zeros((8, 128), F32)

    def heats(n):
        def one(row, heat):
            inv[n, row] = inverse(1.0 + thermal_slope * heat)

        for k in range(ROWS):
            one(RIM + k, part[5 * far + n, k] + g_far[n, k])
        for k in range(RIM):
            one(from_core + k, g_core[n, k] + g_core_far[n, k])
            one(from_tile + k, g_tile[n, k] + g_tile_far[n, k])

    loop(HEATED, heats)
    lower = far.astype(F32)
    halo, none = 7 * (1 - far), 7 * far

    def rim(row, b, up):
        v0[halo, row] = b
        v0[none, row] = zero
        vert[0, row] = up * inv[0, row] * lower

    for k in range(ROWS):
        rim(RIM + k, g_far[HEATED, k], g_far[HEATED + 1, k])
    for k in range(RIM):
        rim(from_core + k, g_core_far[HEATED, k], g_core_far[HEATED + 1, k])
        rim(from_tile + k, g_tile_far[HEATED, k], g_tile_far[HEATED + 1, k])
    for row in range(EXT):
        for edge in (0, 7):
            v1[edge, row] = zero
            v2[edge, row] = zero

    def fields(o):
        def one(row, b, g, up, gr):
            warm = inv[o + far, row]
            v0[o + 1, row] = b
            lat[o, row] = g * warm
            vert[o + 1, row] = up * warm
            ground[o, row] = gr

        for k in range(ROWS):
            one(RIM + k, *[a6[ch, o, k] for ch in range(4)])
        for k in range(RIM):
            one(from_core + k, *[g_core[HEATED + ch * HALF + o, k] for ch in range(4)])
            one(from_tile + k, *[g_tile[HEATED + ch * HALF + o, k] for ch in range(4)])

    loop(HALF, fields)
    last = (sub == 7) & (lane == 127)

    def edges(o):
        for row in range(EXT - 1):
            row_edge[o, row] = harmonic(lat[o, row], lat[o, row + 1])
        for row in range(1, EXT - 1):
            here = lat[o, row]
            ce = jnp.where(last, 0.0, harmonic(here, after(here, lane)))
            col_edge[o, row] = ce
            diag[o, row] = (
                ground[o, row] + vert[o + 1, row] + vert[o, row]
                + row_edge[o, row - 1] + row_edge[o, row] + ce + before(ce, lane)
            )

    loop(HALF, edges)

    def first(o):
        for row in range(1, EXT - 1):
            v1[o + 1, row] = apply(v0, o, row, diag, row_edge, col_edge, vert, lane)

    loop(HALF, first)

    def second(o):
        for row in range(2, EXT - 2):
            v2[o + 1, row] = apply(v1, o, row, diag, row_edge, col_edge, vert, lane)

    loop(HALF, second)
    edge = 5 * (1 - far) + 1
    for k in range(EXT - 4):
        s_basis[0, k] = v1[edge, 2 + k]
        s_basis[1, k] = v2[edge, 2 + k]


def moments_kernel(v0, v1, v2, diag, row_edge, col_edge, vert, got, w2, out):
    far, _ = place()
    _, lane = iotas()

    def copy(n):
        for row in range(2, EXT - 2):
            w2[n, row] = v2[n, row]

    loop(HALF + 2, copy)
    edge, halo = 5 * (1 - far) + 1, 7 * (1 - far)
    for k in range(EXT - 4):
        row = 2 + k
        link = vert[6 * (1 - far), row]
        w2[edge, row] = v2[edge, row] - link * got[0, k]
        w2[halo, row] = got[1, k] - link * v1[edge, row]

    def body(o, sums):
        sums = list(sums)
        for row in range(RIM, RIM + ROWS):
            a, b, c = v0[o + 1, row], v1[o + 1, row], w2[o + 1, row]
            d = apply(w2, o, row, diag, row_edge, col_edge, vert, lane)
            for n, term in enumerate((a * a, a * b, b * b, b * c, c * c, c * d)):
                sums[n] = sums[n] + term
        return tuple(sums)

    sums = lax.fori_loop(0, HALF, body, (jnp.zeros((8, 128), F32),) * 6)
    for n in range(6):
        out[0, pl.ds(n, 1), :] = jnp.full((1, 128), jnp.sum(sums[n]), F32)
    out[0, pl.ds(6, 2), :] = jnp.zeros((2, 128), F32)
    out[1] = jnp.zeros((8, 128), F32)


def two_sum(a, b):
    s = a + b
    t = s - a
    return s, (a - (s - t)) + (b - t)


def two_prod(a, b):
    def split(v):
        t = v * 4097.0
        high = t - (t - v)
        return high, v - high

    p = a * b
    (ah, al), (bh, bl) = split(a), split(b)
    return p, ((ah * bh - p) + ah * bl + al * bh) + al * bl


def pair_add(a, b):
    s, e = two_sum(a[0], b[0])
    e = e + (a[1] + b[1])
    high = s + e
    return high, e - (high - s)


def pair_mul(a, b):
    p, e = two_prod(a[0], b[0])
    e = e + (a[0] * b[1] + a[1] * b[0])
    high = p + e
    return high, e - (high - p)


def pair_neg(a):
    return -a[0], -a[1]


def pair_div(a, b):
    q = a[0] / b[0]
    r = pair_add(a, pair_neg(pair_mul(b, (q, jnp.zeros_like(q)))))
    q2 = (r[0] + r[1]) / b[0]
    high = q + q2
    return high, q2 - (high - q)


def coefficients(m):
    mean, m2, m3, m4, m5 = [pair_div(v, m[0]) for v in m[1:]]
    low = pair_neg(mean)

    def lowered(seq):
        return [pair_add(b, pair_mul(low, a)) for a, b in zip(seq, seq[1:])]

    one = (jnp.ones_like(mean[0]), jnp.zeros_like(mean[0]))
    seq = [one, mean, m2, m3, m4, m5]
    seq = lowered(seq)
    central = []
    for power in range(2, 6):
        seq = lowered(seq)
        central.append(seq[0])
    c2, c3, c4, c5 = [v[0] + v[1] for v in central]
    s = mean[0] + mean[1]
    ok1 = c2 > 3e-8 * s * s
    c2 = jnp.where(ok1, c2, 1.0)
    skew = c3 / c2
    n2 = c4 - skew * c3 - c2 * c2
    ok2 = ok1 & (n2 > 1e-6 * c2 * c2) & (n2 > 3e-8 * (s * s) * (s * s))
    n2 = jnp.where(ok2, n2, 1.0)
    tq = c5 - 2.0 * skew * c4 + (skew * skew - 2.0 * c2) * c3 + 2.0 * skew * c2 * c2
    a2 = s + tq / n2
    a1 = s + skew
    b1, b2 = c2, n2 / c2
    d0 = s
    d1 = a1 - b1 / d0
    d2 = a2 - b2 / d1
    y0 = 1.0 / d0
    y1 = jnp.where(ok1, -y0 / d1, 0.0)
    y2 = jnp.where(ok2, -y1 / d2, 0.0)
    z2 = y2
    z1 = y1 - jnp.where(ok2, b2 * z2 / d1, 0.0)
    z0 = y0 - jnp.where(ok1, b1 * z1 / d0, 0.0)
    k2 = z2
    k1 = z1 - z2 * (skew + 2.0 * s)
    k0 = z0 - z1 * s + z2 * (s * s + skew * s - c2)
    return k0 * SCALE, k1 * SCALE, k2 * SCALE


def power_kernel(
    total, v0, v1, w2, diag, row_edge, col_edge, vert, ground, got,
    power, s_core, s_tile, loss, s_loss, volts,
):
    far, core = place()
    _, lane = iotas()
    spread = [
        (
            jnp.broadcast_to(total[0, pl.ds(n, 1), :], (8, 128)),
            jnp.broadcast_to(total[1, pl.ds(n, 1), :], (8, 128)),
        )
        for n in range(6)
    ]
    c0, c1, c2 = coefficients(spread)
    halo = 7 * (1 - far)

    def combine(n):
        for row in range(2, EXT - 2):
            volts[n, row] = c0 * v0[n, row] + c1 * v1[n, row] + c2 * w2[n, row]

    loop(HALF + 2, combine)
    for k in range(EXT - 4):
        row = 2 + k
        volts[halo, row] = c0 * v0[halo, row] + c1 * got[0, k] + c2 * w2[halo, row]

    def body(o):
        for k in range(ROWS):
            row = RIM + k
            x = volts[o + 1, row]
            near = after(x, lane) - x
            q = col_edge[o, row] * near * near
            q = q + before(q, lane)
            for edge, other in (
                (row_edge[o, row - 1], volts[o + 1, row - 1]),
                (row_edge[o, row], volts[o + 1, row + 1]),
                (vert[o + 1, row], volts[o + 2, row]),
                (vert[o, row], volts[o, row]),
            ):
                d = x - other
                q = q + edge * d * d
            power[o, k] = 16.0 * ground[o, row] * x * x + 8.0 * q

    loop(HALF, body)
    to_core, to_tile = (ROWS - RIM) * (1 - core), (ROWS - RIM) * core

    def sides(o):
        for k in range(RIM):
            s_core[o, k] = power[o, to_core + k]
            s_tile[o, k] = power[o, to_tile + k]

    loop(HALF, sides)

    def outs(n):
        for k in range(ROWS):
            loss[n, k] = volts[1 + OWN * core + n, RIM + k]
            s_loss[n, k] = volts[1 + OWN * (1 - core) + n, RIM + k]

    loop(OWN, outs)


def slab_rim_kernel(t_own, t_got, k_own, k_got, s_core, s_tile):
    _, core = place()
    to_core, to_tile = (ROWS - SWEEPS) * (1 - core), (ROWS - SWEEPS) * core

    def body(n):
        for f, (own, got) in enumerate(((t_own, t_got), (k_own, k_got))):
            for ref, z in ((own, DEEP * core + n), (got, DEEP * (1 - core) + n)):
                for k in range(SWEEPS):
                    s_core[f, z, k] = ref[n, to_core + k]
                    s_tile[f, z, k] = ref[n, to_tile + k]

    loop(DEEP, body)


def deep_rows(step):
    return range(step, WIDE - step), sum(WIDE - 2 * k for k in range(1, step))


DEEP_ROWS = deep_rows(SWEEPS + 1)[1]


def slab_deep_kernel(t_own, t_got, k_own, k_got, g_core, g_tile, s_far):
    far, core = place()

    def side(half, number):
        fields = (t_own, k_own) if number == 1 - half else (t_got, k_got)
        top, bottom = (g_core, g_tile) if number else (g_tile, g_core)
        for step in range(1, SWEEPS + 1):
            rows, start = deep_rows(step)
            n = step - 1 if half else DEEP - step
            z = step - 1 if half else SLAB - step
            for i, row in enumerate(rows):
                for f in range(2):
                    if row < SWEEPS:
                        s_far[f, start + i] = top[f, z, row]
                    elif row < SWEEPS + ROWS:
                        s_far[f, start + i] = fields[f][n, row - SWEEPS]
                    else:
                        s_far[f, start + i] = bottom[f, z, row - SWEEPS - ROWS]

    for half in range(2):
        for number in range(2):
            pl.when((far == half) & (core == number))(functools.partial(side, half, number))


def row_edges_of(n, rows, cond, row_edge):
    for row in rows:
        row_edge[n, row] = harmonic(cond[n, row], cond[n, row + 1])


def col_edges_of(n, rows, cond, col_edge):
    sub, lane = iotas()
    last = (sub == 7) & (lane == 127)
    for row in rows:
        here = cond[n, row]
        col_edge[n, row] = jnp.where(last, 0.0, harmonic(here, after(here, lane)))


def deep_edges_of(n, rows, cond, deep_edge):
    for row in rows:
        deep_edge[n + 1, row] = harmonic(cond[n, row], cond[n + 1, row])


def turns_of(n, rows, deep_edge, row_edge, col_edge, turn):
    _, lane = iotas()
    for row in rows:
        ce = col_edge[n, row]
        turn[n, row] = inverse(
            sink_level + deep_edge[n, row] + deep_edge[n + 1, row]
            + row_edge[n, row - 1] + row_edge[n, row] + ce + before(ce, lane)
        )


OUTER = (*range(1, SWEEPS), *range(SWEEPS + ROWS, WIDE - 1))


def slab_inner_kernel(t_own, t_got, k_own, k_got, warm, cond, deep_edge, row_edge, col_edge, turn):
    far, core = place()
    zero = jnp.zeros((8, 128), F32)
    base = SWEEPS * far

    def body(n):
        for own, got, out, up in ((t_own, t_got, warm, 1), (k_own, k_got, cond, 0)):
            for ref, z in ((own, DEEP * core + n), (got, DEEP * (1 - core) + n)):
                for k in range(ROWS):
                    out[up + base + z, SWEEPS + k] = ref[n, k]

    loop(DEEP, body)
    for row in range(WIDE):
        for n in (0, THICK + 1):
            warm[n, row] = zero
        for n in (0, THICK):
            deep_edge[n, row] = zero
    mid = range(SWEEPS, SWEEPS + ROWS)

    def between(z):
        deep_edges_of(base + z, mid, cond, deep_edge)

    loop(SLAB - 1, between)

    def level(z):
        row_edges_of(base + z, mid[:-1], cond, row_edge)
        col_edges_of(base + z, mid, cond, col_edge)

    loop(SLAB, level)

    def turns(z):
        turns_of(base + 1 + z, mid[1:-1], deep_edge, row_edge, col_edge, turn)

    loop(SLAB - 2, turns)


def slab_outer_kernel(
    warm_in, cond_in, deep_in, row_in, col_in, turn_in, g_core, g_tile, g_far,
    warm, cond, deep_edge, row_edge, col_edge, turn,
):
    far, core = place()
    zero = jnp.zeros((8, 128), F32)
    base = SWEEPS * far
    from_core, from_tile = (WIDE - SWEEPS) * (1 - core), (WIDE - SWEEPS) * core

    def body(z):
        for f, out, up in ((0, warm, 1), (1, cond, 0)):
            for k in range(SWEEPS):
                out[up + base + z, from_core + k] = g_core[f, z, k]
                out[up + base + z, from_tile + k] = g_tile[f, z, k]

    loop(SLAB, body)
    for step in range(1, SWEEPS + 1):
        at = jnp.where(far == 0, SLAB + step - 1, SWEEPS - step)
        rows, start = deep_rows(step)
        for f, out, up in ((0, warm, 1), (1, cond, 0)):
            for row in range(WIDE):
                out[up + at, row] = g_far[f, start + row - step] if row in rows else zero
    every = range(1, WIDE - 1)

    def between(n):
        deep_edges_of(n, OUTER, cond, deep_edge)

    loop(THICK - 1, between)

    def meeting(i):
        deep_edges_of((SLAB - 1) * (1 - far) + i, range(SWEEPS, SWEEPS + ROWS), cond, deep_edge)

    loop(SWEEPS, meeting)

    def level(z):
        row_edges_of(base + z, (*range(SWEEPS), *range(SWEEPS + ROWS - 1, WIDE - 1)), cond, row_edge)
        col_edges_of(base + z, OUTER, cond, col_edge)

    loop(SLAB, level)

    def halo_level(i):
        n = SLAB * (1 - far) + i
        row_edges_of(n, range(WIDE - 1), cond, row_edge)
        col_edges_of(n, every, cond, col_edge)

    loop(SWEEPS, halo_level)

    def turns(z):
        rows = (*range(1, SWEEPS + 1), *range(SWEEPS + ROWS - 1, WIDE - 1))
        turns_of(base + z, rows, deep_edge, row_edge, col_edge, turn)

    loop(SLAB, turns)

    def more_turns(i):
        turns_of((SLAB - 1) * (1 - far) + far + i, every, deep_edge, row_edge, col_edge, turn)

    loop(SWEEPS, more_turns)
    turns_of(0, every, deep_edge, row_edge, col_edge, turn)
    turns_of(THICK - 1, every, deep_edge, row_edge, col_edge, turn)


def relax(n, src, rows, put, source, deep_edge, row_edge, col_edge, turn, lane):
    above, here, e_above = src[n + 1, rows[0] - 1], src[n + 1, rows[0]], row_edge[n, rows[0] - 1]
    for row in rows:
        under, e_under, ce = src[n + 1, row + 1], row_edge[n, row], col_edge[n, row]
        flow = source[n, row] + ce * after(here, lane) + before(ce * here, lane)
        flow = flow + e_above * above + e_under * under
        flow = flow + deep_edge[n, row] * src[n, row] + deep_edge[n + 1, row] * src[n + 2, row]
        put(row, flow * turn[n, row])
        above, here, e_above = here, under, e_under


def sweeps_kernel(
    split, weights, power, p_far, p_core, p_core_far, p_tile, p_tile_far,
    warm, deep_edge, row_edge, col_edge, turn,
    out, s_out, final, s_final,
    joule, source, one, two,
):
    far, core = place()
    _, lane = iotas()
    zero = jnp.zeros((8, 128), F32)
    from_core = 1 + (EXT - RIM) * (1 - core)
    from_tile = 1 + (EXT - RIM) * core

    def gather(o):
        for layer, mid, by_core, by_tile in (
            (HALF * far + o, power, p_core, p_tile),
            (HALF * (1 - far) + o, p_far, p_core_far, p_tile_far),
        ):
            for k in range(ROWS):
                joule[layer, SWEEPS + k] = mid[o, k]
            for k in range(RIM):
                joule[layer, from_core + k] = by_core[o, k]
                joule[layer, from_tile + k] = by_tile[o, k]
            joule[layer, 0] = zero
            joule[layer, WIDE - 1] = zero

    loop(HALF, gather)
    base = (SLAB - SWEEPS) * far

    def sources(block):
        field = [[joule[layer, block * 4 + k] for k in range(4)] for layer in range(LAYERS)]

        def depth(n, carry):
            total = [zero] * 4
            for layer in range(LAYERS):
                w = split[layer, base + n]
                total = [total[k] + w * field[layer][k] for k in range(4)]
            for k in range(4):
                source[n, block * 4 + k] = total[k]
            return carry

        lax.fori_loop(0, THICK, depth, 0, unroll=4)

    loop(WIDE // 4, sources)
    for ref in (one, two):
        for row in range(WIDE):
            ref[0, row] = zero
            ref[THICK + 1, row] = zero

    fields = (source, deep_edge, row_edge, col_edge, turn, lane)
    for sweep, src, dst in ((1, warm, one), (2, one, two), (3, two, one)):

        def step(i, sweep=sweep, src=src, dst=dst):
            n = sweep * far + i

            def put(row, value):
                dst[n + 1, row] = value

            relax(n, src, range(sweep, WIDE - sweep), put, *fields)

        loop(THICK - sweep, step, 5)
    for ref, half in ((out, core), (s_out, 1 - core)):

        def final_step(i, ref=ref, half=half):
            def put(row, value):
                ref[i, row - SWEEPS] = value

            relax(SWEEPS * far + DEEP * half + i, one, range(SWEEPS, SWEEPS + ROWS), put, *fields)

        loop(DEEP, final_step)
    weigh(
        weights,
        ((out, 0, SLAB * far + DEEP * core), (s_out, 0, SLAB * far + DEEP * (1 - core))),
        final,
    )

    def sends(o):
        for k in range(ROWS):
            s_final[o, k] = final[HALF * (1 - far) + o, k]

    loop(HALF, sends)


def update_kernel(final, got, a6, mine, send):
    far, core = place()

    def body(n):
        for half, out in ((core, mine), (1 - core, send)):
            o = OWN * half + n
            for k in range(ROWS):
                heat = final[HALF * far + o, k] + got[o, k]
                out[n, k] = (16.0 * a6[1, o, k]) * inverse(1.0 + thermal_slope * heat)

    loop(OWN, body)


def unpack_kernel(own, got, out):
    _, core = place()

    def body(n):
        for k in range(ROWS):
            out[n, core * 2 + k // 8, pl.ds(k % 8, 8, stride=8), :] = own[n, k]
            out[n, (1 - core) * 2 + k // 8, pl.ds(k % 8, 8, stride=8), :] = got[n, k]

    loop(own.shape[0], body)


def unpack(own, got):
    n = own.shape[0]
    out = jax.ShapeDtypeStruct((n, 4, 64, 128), F32)
    return raw_back(call(unpack_kernel, out, cost=n / 10, raw_out=True)(own, got))


def pack(value):
    n = value.shape[0]
    return call(pack_kernel, [shaped(n, ROWS)] * 2, cost=2, raw_in=True)(raw_view(value))


def to_core(value):
    return lax.ppermute(value, "therm", [(i, i ^ 1) for i in range(4)])


def to_far(value):
    return lax.ppermute(value, "therm", [(i, i ^ 2) for i in range(4)])


def to_core_far(value):
    return lax.ppermute(value, "therm", [(i, i ^ 3) for i in range(4)])


def to_tile(value, cross=0):
    pairs = []
    for t in range(lax.axis_size("tile") - 1):
        for half in range(2):
            low = 4 * t + 2 * half + 1
            high = 4 * (t + 1) + 2 * (half ^ cross)
            pairs += [(low, high), (high, low)]
    return lax.ppermute(value, ("tile", "therm"), pairs)


def add_pairs(a, b):
    high, low = pair_add((a[0], a[1]), (b[0], b[1]))
    return jnp.stack([high, low])


def along_core_and_x(values):
    values = add_pairs(values, to_core(values))
    peers = []
    for bits in (2, 3, 1):
        pairs = [
            (4 * t + h, 4 * (t ^ (bits & 1)) + (h ^ (bits & 2)))
            for t in range(lax.axis_size("tile"))
            for h in range(4)
        ]
        peers.append(lax.ppermute(values, ("tile", "therm"), pairs))
    for peer in peers:
        values = add_pairs(values, peer)
    return values


def along_tile(values, unit):
    peers = [
        lax.ppermute(values, "tile", [(t, t ^ (unit * k)) for t in range(lax.axis_size("tile"))])
        for k in (2, 1, 3)
    ]
    for peer in peers:
        values = add_pairs(values, peer)
    return values


def tied(value, to):
    return lax.optimization_barrier((value, to))[0]


def per_device(
    sink_current,
    metal_category,
    upward_link_flag,
    supply_contact_flag,
    baseline_admittance,
    beginning_warmth,
    cell_diffusivity,
    dissipation_split,
    probe_weighting,
):
    weights, split = probe_weighting, dissipation_split.T
    t_own, t_send = pack(beginning_warmth)
    t_got = to_core(t_send)
    a_own, a_send = call(pack_args_kernel, [shaped(4 * OWN, ROWS)] * 2, scalars=1, cost=3, raw_in=True)(
        baseline_admittance,
        *[raw_view(v) for v in (sink_current, metal_category, upward_link_flag, supply_contact_flag)],
    )
    a_got = to_core(a_send)
    part = call(heat_kernel, shaped(LAYERS, ROWS), scalars=1, cost=3, room=2)(weights, t_own, t_got)
    a6, s_far, s_core_far, s_tile_far, s_core, s_tile = call(
        merge_kernel,
        [
            shaped(4, HALF, ROWS),
            shaped(HEATED + 2, ROWS),
            shaped(HEATED + 2, RIM),
            shaped(HEATED + 2, RIM),
            shaped(HEATED + 4 * HALF, RIM),
            shaped(HEATED + 4 * HALF, RIM),
        ],
        cost=1.5,
        room=2,
    )(part, a_own, a_got)
    g_far = to_far(s_far)
    g_tile = to_tile(s_tile)
    g_tile_far = to_tile(s_tile_far, 1)
    g_core_far = to_core_far(s_core_far)
    g_core = to_core(s_core)

    k_own, k_send = pack(tied(cell_diffusivity, s_far))

    field = shaped(HALF + 2, EXT)
    coef = shaped(HALF, EXT)
    v0, v1, v2, diag, row_edge, col_edge, vert, ground, s_basis = call(
        basis_kernel,
        [field, field, field, coef, coef, coef, shaped(HALF + 1, EXT), coef, shaped(2, EXT - 4)],
        scratch=((HEATED, EXT), (HALF, EXT)),
        cost=3,
    )(part, a6, g_far, g_core_far, g_tile_far, g_core, g_tile)
    g_basis = to_far(s_basis)
    k_got = to_core(tied(k_send, s_basis))
    rim = shaped(2, SLAB, SWEEPS)
    k_core, k_tile = call(slab_rim_kernel, [rim, rim], cost=0.4)(t_own, t_got, k_own, k_got)
    g_core, g_rim = to_core(k_core), to_tile(k_tile)
    s_deep = call(slab_deep_kernel, shaped(2, DEEP_ROWS), cost=0.3)(t_own, t_got, k_own, k_got, g_core, g_rim)
    w2, sums = call(moments_kernel, [field, shaped(2)], cost=0.9)(
        tied(v0, k_tile), v1, v2, diag, row_edge, col_edge, vert, g_basis
    )
    thick = shaped(THICK, WIDE)
    inner = call(
        slab_inner_kernel, [shaped(THICK + 2, WIDE), thick, shaped(THICK + 1, WIDE), thick, thick, thick], cost=5.5
    )(tied(t_own, sums), t_got, k_own, k_got)
    values = along_core_and_x(sums)
    values, s_deep, inner = lax.optimization_barrier((values, s_deep, inner))
    values = along_tile(values, 2)
    total = along_tile(values, 8)
    total, g_deep = lax.optimization_barrier((total, to_far(s_deep)))

    power, p_core, p_tile, loss, s_loss = call(
        power_kernel,
        [shaped(HALF, ROWS), shaped(HALF, RIM), shaped(HALF, RIM), shaped(OWN, ROWS), shaped(OWN, ROWS)],
        scratch=((HALF + 2, EXT),),
        cost=1.4,
    )(total, v0, v1, w2, diag, row_edge, col_edge, vert, ground, g_basis)
    p_far = to_far(power)
    q_tile = to_tile(p_tile)
    q_tile_far = to_tile(p_tile, 1)
    q_core_far = to_core_far(p_core)
    q_core = to_core(p_core)
    voltage_loss = unpack(loss, to_core(s_loss))

    warm, _, *edges = call(
        slab_outer_kernel,
        [shaped(THICK + 2, WIDE), thick, shaped(THICK + 1, WIDE), thick, thick, thick],
        cost=4,
        alias={i: i for i in range(6)},
    )(*inner, g_core, g_rim, g_deep)
    out, s_out, final, s_final = call(
        sweeps_kernel,
        [shaped(DEEP, ROWS), shaped(DEEP, ROWS), shaped(LAYERS, ROWS), shaped(HALF, ROWS)],
        scratch=((LAYERS, WIDE), (THICK, WIDE), (THICK + 2, WIDE), (THICK + 2, WIDE)),
        scalars=2,
        cost=25,
        room=14,
    )(split, weights, power, p_far, q_core, q_core_far, q_tile, q_tile_far, warm, *edges)
    g_final = to_far(s_final)
    final_warmth = unpack(out, to_core(s_out))
    g_final = tied(g_final, final_warmth)
    mine, s_mine = call(update_kernel, [shaped(OWN, ROWS)] * 2, cost=0.4)(final, g_final, a6)
    updated_admittance = unpack(mine, to_core(s_mine))
    return voltage_loss, final_warmth, updated_admittance


def solution(mesh):
    spread = P("therm", "tile", None)
    return jax.shard_map(
        per_device,
        mesh=mesh,
        in_specs=(spread, spread, spread, spread, P(), spread, spread, P(), P()),
        out_specs=(spread, spread, spread),
        check_vma=False,
    )
```

```python
import functools

import jax
import jax.numpy as jnp
from jax import lax
from jax.experimental import pallas as pl
from jax.experimental.pallas import tpu as pltpu
from jax.sharding import PartitionSpec as P


LAYERS = 12
HALF = LAYERS // 2
OWN = 3
DEPTHS = 64
SLAB = DEPTHS // 2
DEEP = 16
ROWS = 16
RIM = 3
SIDE = 2 * RIM + 2 * (RIM - 1)
EXT = ROWS + 2 * RIM
HEATED = 7
SWEEPS = 4
PARTS = 4
WIDE = ROWS + 2 * SWEEPS
THICK = SLAB + SWEEPS
SCALE = 1.0 / 16.0
TINY = 1e-30

shunt_level = 0.05
pad_conductance = 4.0
via_conductance = 2.0
thermal_slope = 0.2
sink_level = 0.1

F32 = jnp.float32


def place():
    therm = lax.axis_index("therm")
    return therm // 2, therm % 2


def shaped(*dims):
    return jax.ShapeDtypeStruct(dims + (8, 128), F32)


def call(kernel, outs, scratch=(), scalars=0, cost=0, raw_in=False, raw_out=False, room=4, alias={}, hold=lambda i: True):
    def held(out):
        return out if raw_out else pltpu.VMEM(out.shape, out.dtype)

    def run(*args):
        smem = [pl.BlockSpec(memory_space=pltpu.SMEM)] * scalars
        fields = args[scalars:]
        space = pltpu.HBM if raw_in else pltpu.VMEM
        fields = [pltpu.with_memory_space_constraint(v, space) for v in fields]
        own = [(pltpu.VMEM if v.ndim > 1 else pltpu.SMEM)(v.shape, v.dtype) for i, v in enumerate(fields) if hold(i)] if raw_in else []
        own += [pltpu.SemaphoreType.DMA((PARTS + len(fields),))] if raw_in else []
        return pl.pallas_call(
            kernel,
            out_shape=jax.tree.map(held, outs),
            in_specs=smem + [pl.BlockSpec(memory_space=space)] * len(fields),
            input_output_aliases=alias,
            out_specs=jax.tree.map(lambda _: pl.BlockSpec(memory_space=pltpu.VMEM), outs),
            scratch_shapes=[pltpu.VMEM(dims + (8, 128), F32) for dims in scratch] + own,
            compiler_params=pltpu.CompilerParams(vmem_limit_bytes=room * 1024 * 1024),
            cost_estimate=pl.CostEstimate(flops=0, bytes_accessed=int(cost * 3.4e6), transcendentals=0),
        )(*args[:scalars], *fields)

    return run


def raw_view(value):
    n, rows, width = value.shape
    split = value.reshape(n, rows // 8, 8, width // 128, 128).transpose(0, 1, 3, 2, 4)
    return split.reshape(n, rows // 8, 8 * (width // 128), 128)


def raw_back(value):
    n, blocks, high, lanes = value.shape
    split = value.reshape(n, blocks, high // 8, 8, lanes).transpose(0, 1, 3, 2, 4)
    return split.reshape(n, blocks * 8, (high // 8) * lanes)


def at_row(ref, n, chunk, row):
    return ref[n, chunk * 2 + row // 8, pl.ds(row % 8, 8, stride=8), :]


def loop(count, body, unroll=4):
    def step(i, carry):
        body(i)
        return carry

    lax.fori_loop(0, count, step, 0, unroll=min(unroll, count))


def iotas():
    return lax.broadcasted_iota(jnp.int32, (8, 128), 0), lax.broadcasted_iota(jnp.int32, (8, 128), 1)


def after(v, lane):
    r = pltpu.roll(v, 127, 1)
    return jnp.where(lane == 127, pltpu.roll(r, 7, 0), r)


def before(v, lane):
    r = pltpu.roll(v, 1, 1)
    return jnp.where(lane == 0, pltpu.roll(r, 1, 0), r)


def inverse(v):
    r = pl.reciprocal(v, approx=True)
    r = r * (2.0 - v * r)
    return r * (2.0 - v * r)


def harmonic(a, b):
    return a * b * inverse(jnp.maximum(a + b, TINY))


def pack_field(value, held, sems):
    size = value.shape[0] // PARTS
    copies = [
        pltpu.make_async_copy(value.at[pl.ds(p * size, size)], held.at[pl.ds(p * size, size)], sems.at[p])
        for p in range(PARTS)
    ]
    for copy in copies:
        copy.start()

    def finish(own, send):
        _, core = place()
        for p, copy in enumerate(copies):
            copy.wait()

            def body(i, p=p):
                n = p * size + i
                for row in range(ROWS):
                    own[n, row] = at_row(held, n, core, row)
                    send[n, row] = at_row(held, n, 1 - core, row)

            loop(size, body)

    return finish


def pack_kernel(value, own, send, held, sems):
    pack_field(value, held, sems)(own, send)


def first_pack_kernel(
    value, sink, category, link, contact, classes, t_own, t_send, sink_, category_, link_, contact_, table, held, classes_, sems
):
    finish = pack_field(value, held, sems)
    raw = ((classes, classes_), (sink, sink_), (category, category_), (link, link_), (contact, contact_))
    copies = [pltpu.make_async_copy(ref, to, sems.at[PARTS + p]) for p, (ref, to) in enumerate(raw)]
    for copy in copies:
        copy.start()
    finish(t_own, t_send)
    for copy in copies:
        copy.wait()
    for number in range(8):
        table[number] = jnp.full((8, 128), classes_[number] * SCALE, F32)


def pack_args_kernel(sink, category, link, contact, classes, own, send):
    _, core = place()

    def body(n):
        for row in range(ROWS):
            for chunk, out in ((core, own), (1 - core, send)):
                kind = at_row(category, n, chunk, row)
                table = classes[0]
                for number in range(1, 8):
                    table = jnp.where(kind == number, classes[number], table)
                out[n, row] = at_row(sink, n, chunk, row)
                out[OWN + n, row] = table
                out[2 * OWN + n, row] = at_row(link, n, chunk, row).astype(F32) * (via_conductance * SCALE)
                out[3 * OWN + n, row] = at_row(contact, n, chunk, row).astype(F32) * (
                    pad_conductance * SCALE
                ) + (shunt_level * SCALE)

    loop(OWN, body)


def weigh(weights, parts, acc, first_layer=0):
    layers, rows = acc.shape[:2]
    size = 48 // layers

    def block_of(block):
        total = [jnp.zeros((8, 128), F32)] * (size * layers)
        for ref, first, base in parts:

            def step(z, total):
                field = [ref[first + z, block * size + k] for k in range(size)]
                out = []
                for layer in range(layers):
                    w = weights[first_layer + layer, base + z]
                    out += [total[layer * size + k] + w * field[k] for k in range(size)]
                return tuple(out)

            total = lax.fori_loop(0, DEEP, step, tuple(total), unroll=16)
        for layer in range(layers):
            for k in range(size):
                acc[layer, block * size + k] = total[layer * size + k]

    loop(rows // size, block_of, 1)


def heat_kernel(weights, t_own, t_got, part):
    weigh(weights, heat_parts(t_own, t_got), part)


def merge_kernel(part, a_own, a_got, a6, s_far, s_core_far, s_tile_far, s_core, s_tile):
    far, core = place()

    def merge(n):
        for row in range(ROWS):
            for ch in range(4):
                a6[ch, OWN * core + n, row] = a_own[ch * OWN + n, row]
                a6[ch, OWN * (1 - core) + n, row] = a_got[ch * OWN + n, row]

    loop(OWN, merge)
    to_core, to_tile = (ROWS - RIM) * (1 - core), (ROWS - RIM) * core

    def heats(n):
        for row in range(ROWS):
            s_far[n, row] = part[5 * (1 - far) + n, row]
        for k in range(RIM):
            s_core_far[n, k] = part[5 * (1 - far) + n, to_core + k]
            s_tile_far[n, k] = part[5 * (1 - far) + n, to_tile + k]
            s_core[n, k] = part[5 * far + n, to_core + k]
            s_tile[n * RIM + k] = part[5 * far + n, to_tile + k]

    loop(HEATED, heats)
    edge = 5 * (1 - far)
    for n, ch in ((HEATED, 0), (HEATED + 1, 2)):
        for row in range(ROWS):
            s_far[n, row] = a6[ch, edge, row]
        for k in range(RIM):
            s_core_far[n, k] = a6[ch, edge, to_core + k]
            s_tile_far[n, k] = a6[ch, edge, to_tile + k]

    def args(o):
        for ch in range(4):
            for k in range(RIM):
                s_core[HEATED + ch * HALF + o, k] = a6[ch, o, to_core + k]
        first = HEATED * RIM + o * SIDE
        for k in range(RIM):
            s_tile[first + k] = a6[0, o, to_tile + k]
            s_tile[first + RIM + k] = a6[1, o, to_tile + k]
        for k in range(RIM - 1):
            s_tile[first + 2 * RIM + k] = a6[2, o, to_tile + core + k]
            s_tile[first + 3 * RIM - 1 + k] = a6[3, o, to_tile + core + k]

    loop(HALF, args)


def apply(v, o, row, diag, row_edge, col_edge, vert, lane):
    here = v[o + 1, row]
    ce = col_edge[o, row]
    return (
        diag[o, row] * here
        - row_edge[o, row - 1] * v[o + 1, row - 1]
        - row_edge[o, row] * v[o + 1, row + 1]
        - ce * after(here, lane)
        - before(ce * here, lane)
        - vert[o + 1, row] * v[o + 2, row]
        - vert[o, row] * v[o, row]
    )


def basis_kernel(
    part, a6, g_far, g_core_far, g_tile_far, g_core, g_tile,
    v0, v1, v2, diag, row_edge, col_edge, vert, ground, s_basis, inv, lat,
):
    far, core = place()
    sub, lane = iotas()
    from_core, from_tile = (EXT - RIM) * (1 - core), (EXT - RIM) * core
    zero = jnp.zeros((8, 128), F32)

    def heats(n):
        def one(row, heat):
            inv[n, row] = inverse(1.0 + thermal_slope * heat)

        for k in range(ROWS):
            one(RIM + k, part[5 * far + n, k] + g_far[n, k])
        for k in range(RIM):
            one(from_core + k, g_core[n, k] + g_core_far[n, k])
            one(from_tile + k, g_tile[n * RIM + k] + g_tile_far[n, k])

    loop(HEATED, heats)
    lower = far.astype(F32)
    halo, none = 7 * (1 - far), 7 * far

    def rim(row, b, up):
        v0[halo, row] = b
        v0[none, row] = zero
        vert[0, row] = up * inv[0, row] * lower

    for k in range(ROWS):
        rim(RIM + k, g_far[HEATED, k], g_far[HEATED + 1, k])
    for k in range(RIM):
        rim(from_core + k, g_core_far[HEATED, k], g_core_far[HEATED + 1, k])
        rim(from_tile + k, g_tile_far[HEATED, k], g_tile_far[HEATED + 1, k])
    for row in range(EXT):
        for edge in (0, 7):
            v1[edge, row] = zero
            v2[edge, row] = zero

    def fields(o):
        def one(row, b, g, up, gr):
            warm = inv[o + far, row]
            v0[o + 1, row] = b
            lat[o, row] = g * warm
            vert[o + 1, row] = up * warm
            ground[o, row] = gr

        for k in range(ROWS):
            one(RIM + k, *[a6[ch, o, k] for ch in range(4)])
        for k in range(RIM):
            one(from_core + k, *[g_core[HEATED + ch * HALF + o, k] for ch in range(4)])
        first = HEATED * RIM + o * SIDE
        for k in range(RIM):
            v0[o + 1, from_tile + k] = g_tile[first + k]
            lat[o, from_tile + k] = g_tile[first + RIM + k] * inv[o + far, from_tile + k]
        for k in range(RIM - 1):
            row = from_tile + 1 - core + k
            vert[o + 1, row] = g_tile[first + 2 * RIM + k] * inv[o + far, row]
            ground[o, row] = g_tile[first + 3 * RIM - 1 + k]

    loop(HALF, fields)
    last = (sub == 7) & (lane == 127)

    def edges(o):
        for row in range(EXT - 1):
            row_edge[o, row] = harmonic(lat[o, row], lat[o, row + 1])
        for row in range(1, EXT - 1):
            here = lat[o, row]
            ce = jnp.where(last, 0.0, harmonic(here, after(here, lane)))
            col_edge[o, row] = ce
            diag[o, row] = (
                ground[o, row] + vert[o + 1, row] + vert[o, row]
                + row_edge[o, row - 1] + row_edge[o, row] + ce + before(ce, lane)
            )

    loop(HALF, edges)

    def first(o):
        for row in range(1, EXT - 1):
            v1[o + 1, row] = apply(v0, o, row, diag, row_edge, col_edge, vert, lane)

    loop(HALF, first)

    def second(o):
        for row in range(2, EXT - 2):
            v2[o + 1, row] = apply(v1, o, row, diag, row_edge, col_edge, vert, lane)

    loop(HALF, second)
    edge = 5 * (1 - far) + 1
    for k in range(EXT - 4):
        s_basis[0, k] = v1[edge, 2 + k]
        s_basis[1, k] = v2[edge, 2 + k]


def moments_kernel(v0, v1, v2, diag, row_edge, col_edge, vert, got, w2, out):
    far, _ = place()
    _, lane = iotas()

    def copy(n):
        for row in range(2, EXT - 2):
            w2[n, row] = v2[n, row]

    loop(HALF + 2, copy)
    edge, halo = 5 * (1 - far) + 1, 7 * (1 - far)
    for k in range(EXT - 4):
        row = 2 + k
        link = vert[6 * (1 - far), row]
        w2[edge, row] = v2[edge, row] - link * got[0, k]
        w2[halo, row] = got[1, k] - link * v1[edge, row]

    def body(o, sums):
        sums = list(sums)
        for row in range(RIM, RIM + ROWS):
            a, b, c = v0[o + 1, row], v1[o + 1, row], w2[o + 1, row]
            d = apply(w2, o, row, diag, row_edge, col_edge, vert, lane)
            for n, term in enumerate((a * a, a * b, b * b, b * c, c * c, c * d)):
                sums[n] = sums[n] + term
        return tuple(sums)

    sums = lax.fori_loop(0, HALF, body, (jnp.zeros((8, 128), F32),) * 6)
    for n in range(6):
        out[0, pl.ds(n, 1), :] = jnp.full((1, 128), jnp.sum(sums[n]), F32)
    out[0, pl.ds(6, 2), :] = jnp.zeros((2, 128), F32)
    out[1] = jnp.zeros((8, 128), F32)


def two_sum(a, b):
    s = a + b
    t = s - a
    return s, (a - (s - t)) + (b - t)


def two_prod(a, b):
    def split(v):
        t = v * 4097.0
        high = t - (t - v)
        return high, v - high

    p = a * b
    (ah, al), (bh, bl) = split(a), split(b)
    return p, ((ah * bh - p) + ah * bl + al * bh) + al * bl


def pair_add(a, b):
    s, e = two_sum(a[0], b[0])
    e = e + (a[1] + b[1])
    high = s + e
    return high, e - (high - s)


def pair_mul(a, b):
    p, e = two_prod(a[0], b[0])
    e = e + (a[0] * b[1] + a[1] * b[0])
    high = p + e
    return high, e - (high - p)


def pair_neg(a):
    return -a[0], -a[1]


def pair_div(a, b):
    q = a[0] / b[0]
    r = pair_add(a, pair_neg(pair_mul(b, (q, jnp.zeros_like(q)))))
    q2 = (r[0] + r[1]) / b[0]
    high = q + q2
    return high, q2 - (high - q)


def coefficients(m):
    mean, m2, m3, m4, m5 = [pair_div(v, m[0]) for v in m[1:]]
    low = pair_neg(mean)

    def lowered(seq):
        return [pair_add(b, pair_mul(low, a)) for a, b in zip(seq, seq[1:])]

    one = (jnp.ones_like(mean[0]), jnp.zeros_like(mean[0]))
    seq = [one, mean, m2, m3, m4, m5]
    seq = lowered(seq)
    central = []
    for power in range(2, 6):
        seq = lowered(seq)
        central.append(seq[0])
    c2, c3, c4, c5 = [v[0] + v[1] for v in central]
    s = mean[0] + mean[1]
    ok1 = c2 > 3e-8 * s * s
    c2 = jnp.where(ok1, c2, 1.0)
    skew = c3 / c2
    n2 = c4 - skew * c3 - c2 * c2
    ok2 = ok1 & (n2 > 1e-6 * c2 * c2) & (n2 > 3e-8 * (s * s) * (s * s))
    n2 = jnp.where(ok2, n2, 1.0)
    tq = c5 - 2.0 * skew * c4 + (skew * skew - 2.0 * c2) * c3 + 2.0 * skew * c2 * c2
    a2 = s + tq / n2
    a1 = s + skew
    b1, b2 = c2, n2 / c2
    d0 = s
    d1 = a1 - b1 / d0
    d2 = a2 - b2 / d1
    y0 = 1.0 / d0
    y1 = jnp.where(ok1, -y0 / d1, 0.0)
    y2 = jnp.where(ok2, -y1 / d2, 0.0)
    z2 = y2
    z1 = y1 - jnp.where(ok2, b2 * z2 / d1, 0.0)
    z0 = y0 - jnp.where(ok1, b1 * z1 / d0, 0.0)
    k2 = z2
    k1 = z1 - z2 * (skew + 2.0 * s)
    k0 = z0 - z1 * s + z2 * (s * s + skew * s - c2)
    return k0 * SCALE, k1 * SCALE, k2 * SCALE


def power_kernel(
    total, v0, v1, w2, diag, row_edge, col_edge, vert, ground, got,
    power, s_core, s_tile, loss, s_loss, volts,
):
    far, core = place()
    _, lane = iotas()
    spread = [
        (
            jnp.broadcast_to(total[0, pl.ds(n, 1), :], (8, 128)),
            jnp.broadcast_to(total[1, pl.ds(n, 1), :], (8, 128)),
        )
        for n in range(6)
    ]
    c0, c1, c2 = coefficients(spread)
    halo = 7 * (1 - far)

    def combine(n):
        for row in range(2, EXT - 2):
            volts[n, row] = c0 * v0[n, row] + c1 * v1[n, row] + c2 * w2[n, row]

    loop(HALF + 2, combine)
    for k in range(EXT - 4):
        row = 2 + k
        volts[halo, row] = c0 * v0[halo, row] + c1 * got[0, k] + c2 * w2[halo, row]

    def body(o):
        for k in range(ROWS):
            row = RIM + k
            x = volts[o + 1, row]
            near = after(x, lane) - x
            q = col_edge[o, row] * near * near
            q = q + before(q, lane)
            for edge, other in (
                (row_edge[o, row - 1], volts[o + 1, row - 1]),
                (row_edge[o, row], volts[o + 1, row + 1]),
                (vert[o + 1, row], volts[o + 2, row]),
                (vert[o, row], volts[o, row]),
            ):
                d = x - other
                q = q + edge * d * d
            power[o, k] = 16.0 * ground[o, row] * x * x + 8.0 * q

    loop(HALF, body)
    to_core, to_tile = (ROWS - RIM) * (1 - core), (ROWS - RIM) * core

    def sides(o):
        for k in range(RIM):
            s_core[o, k] = power[o, to_core + k]
            s_tile[o, k] = power[o, to_tile + k]

    loop(HALF, sides)

    def outs(n):
        for k in range(ROWS):
            loss[n, k] = volts[1 + OWN * core + n, RIM + k]
            s_loss[n, k] = volts[1 + OWN * (1 - core) + n, RIM + k]

    loop(OWN, outs)


def slab_rim_kernel(t_own, t_got, k_own, k_got, s_core, s_tile):
    _, core = place()
    to_core, to_tile = (ROWS - SWEEPS) * (1 - core), (ROWS - SWEEPS) * core

    def body(n):
        for f, (own, got) in enumerate(((t_own, t_got), (k_own, k_got))):
            for ref, z in ((own, DEEP * core + n), (got, DEEP * (1 - core) + n)):
                for k in range(SWEEPS):
                    s_core[f, z, k] = ref[n, to_core + k]
                    s_tile[f, z, k] = ref[n, to_tile + k]

    loop(DEEP, body)


def deep_rows(step):
    return range(step, WIDE - step), sum(WIDE - 2 * k for k in range(1, step))


DEEP_ROWS = deep_rows(SWEEPS + 1)[1]


def slab_deep_kernel(t_own, t_got, k_own, k_got, g_core, g_tile, s_far):
    far, core = place()

    def side(half, number):
        fields = (t_own, k_own) if number == 1 - half else (t_got, k_got)
        top, bottom = (g_core, g_tile) if number else (g_tile, g_core)
        for step in range(1, SWEEPS + 1):
            rows, start = deep_rows(step)
            n = step - 1 if half else DEEP - step
            z = step - 1 if half else SLAB - step
            for i, row in enumerate(rows):
                for f in range(2):
                    if row < SWEEPS:
                        s_far[f, start + i] = top[f, z, row]
                    elif row < SWEEPS + ROWS:
                        s_far[f, start + i] = fields[f][n, row - SWEEPS]
                    else:
                        s_far[f, start + i] = bottom[f, z, row - SWEEPS - ROWS]

    for half in range(2):
        for number in range(2):
            pl.when((far == half) & (core == number))(functools.partial(side, half, number))


def row_edges_of(n, rows, cond, row_edge):
    for row in rows:
        row_edge[n, row] = harmonic(cond[n, row], cond[n, row + 1])


def col_edges_of(n, rows, cond, col_edge):
    sub, lane = iotas()
    last = (sub == 7) & (lane == 127)
    for row in rows:
        here = cond[n, row]
        col_edge[n, row] = jnp.where(last, 0.0, harmonic(here, after(here, lane)))


def deep_edges_of(n, rows, cond, deep_edge):
    for row in rows:
        deep_edge[n + 1, row] = harmonic(cond[n, row], cond[n + 1, row])


def turns_of(n, rows, deep_edge, row_edge, col_edge, turn):
    _, lane = iotas()
    for row in rows:
        ce = col_edge[n, row]
        turn[n, row] = inverse(
            sink_level + deep_edge[n, row] + deep_edge[n + 1, row]
            + row_edge[n, row - 1] + row_edge[n, row] + ce + before(ce, lane)
        )


OUTER = (*range(1, SWEEPS), *range(SWEEPS + ROWS, WIDE - 1))


def slab_inner_kernel(t_own, t_got, k_own, k_got, warm, cond, deep_edge, row_edge, col_edge, turn):
    far, core = place()
    zero = jnp.zeros((8, 128), F32)
    base = SWEEPS * far

    def body(n):
        for own, got, out, up in ((t_own, t_got, warm, 1), (k_own, k_got, cond, 0)):
            for ref, z in ((own, DEEP * core + n), (got, DEEP * (1 - core) + n)):
                for k in range(ROWS):
                    out[up + base + z, SWEEPS + k] = ref[n, k]

    loop(DEEP, body)
    for row in range(WIDE):
        for n in (0, THICK + 1):
            warm[n, row] = zero
        for n in (0, THICK):
            deep_edge[n, row] = zero
    mid = range(SWEEPS, SWEEPS + ROWS)

    def between(z):
        deep_edges_of(base + z, mid, cond, deep_edge)

    loop(SLAB - 1, between)

    def level(z):
        row_edges_of(base + z, mid[:-1], cond, row_edge)
        col_edges_of(base + z, mid, cond, col_edge)

    loop(SLAB, level)

    def turns(z):
        turns_of(base + 1 + z, mid[1:-1], deep_edge, row_edge, col_edge, turn)

    loop(SLAB - 2, turns)


def slab_outer_kernel(
    warm_in, cond_in, deep_in, row_in, col_in, turn_in, g_core, g_tile, g_far,
    warm, cond, deep_edge, row_edge, col_edge, turn,
):
    far, core = place()
    zero = jnp.zeros((8, 128), F32)
    base = SWEEPS * far
    from_core, from_tile = (WIDE - SWEEPS) * (1 - core), (WIDE - SWEEPS) * core

    def body(z):
        for f, out, up in ((0, warm, 1), (1, cond, 0)):
            for k in range(SWEEPS):
                out[up + base + z, from_core + k] = g_core[f, z, k]
                out[up + base + z, from_tile + k] = g_tile[f, z, k]

    loop(SLAB, body)
    for step in range(1, SWEEPS + 1):
        at = jnp.where(far == 0, SLAB + step - 1, SWEEPS - step)
        rows, start = deep_rows(step)
        for f, out, up in ((0, warm, 1), (1, cond, 0)):
            for row in range(WIDE):
                out[up + at, row] = g_far[f, start + row - step] if row in rows else zero
    every = range(1, WIDE - 1)

    def between(n):
        deep_edges_of(n, OUTER, cond, deep_edge)

    loop(THICK - 1, between)

    def meeting(i):
        deep_edges_of((SLAB - 1) * (1 - far) + i, range(SWEEPS, SWEEPS + ROWS), cond, deep_edge)

    loop(SWEEPS, meeting)

    def level(z):
        row_edges_of(base + z, (*range(SWEEPS), *range(SWEEPS + ROWS - 1, WIDE - 1)), cond, row_edge)
        col_edges_of(base + z, OUTER, cond, col_edge)

    loop(SLAB, level)

    def halo_level(i):
        n = SLAB * (1 - far) + i
        row_edges_of(n, range(WIDE - 1), cond, row_edge)
        col_edges_of(n, every, cond, col_edge)

    loop(SWEEPS, halo_level)

    def turns(z):
        rows = (*range(1, SWEEPS + 1), *range(SWEEPS + ROWS - 1, WIDE - 1))
        turns_of(base + z, rows, deep_edge, row_edge, col_edge, turn)

    loop(SLAB, turns)

    def more_turns(i):
        turns_of((SLAB - 1) * (1 - far) + far + i, every, deep_edge, row_edge, col_edge, turn)

    loop(SWEEPS, more_turns)
    turns_of(0, every, deep_edge, row_edge, col_edge, turn)
    turns_of(THICK - 1, every, deep_edge, row_edge, col_edge, turn)


def relax(n, src, rows, put, source, deep_edge, row_edge, col_edge, turn, lane):
    above, here, e_above = src[n + 1, rows[0] - 1], src[n + 1, rows[0]], row_edge[n, rows[0] - 1]
    for row in rows:
        under, e_under, ce = src[n + 1, row + 1], row_edge[n, row], col_edge[n, row]
        flow = source[n, row] + ce * after(here, lane) + before(ce * here, lane)
        flow = flow + e_above * above + e_under * under
        flow = flow + deep_edge[n, row] * src[n, row] + deep_edge[n + 1, row] * src[n + 2, row]
        put(row, flow * turn[n, row])
        above, here, e_above = here, under, e_under


def sweeps_kernel(
    split, weights, power, p_far, p_core, p_core_far, p_tile, p_tile_far,
    warm, deep_edge, row_edge, col_edge, turn,
    out, s_out, s_final,
    joule, source, one, two,
):
    far, core = place()
    _, lane = iotas()
    zero = jnp.zeros((8, 128), F32)
    from_core = 1 + (EXT - RIM) * (1 - core)
    from_tile = 1 + (EXT - RIM) * core

    def gather(o):
        for layer, mid, by_core, by_tile in (
            (HALF * far + o, power, p_core, p_tile),
            (HALF * (1 - far) + o, p_far, p_core_far, p_tile_far),
        ):
            for k in range(ROWS):
                joule[layer, SWEEPS + k] = mid[o, k]
            for k in range(RIM):
                joule[layer, from_core + k] = by_core[o, k]
                joule[layer, from_tile + k] = by_tile[o, k]
            joule[layer, 0] = zero
            joule[layer, WIDE - 1] = zero

    loop(HALF, gather)
    base = (SLAB - SWEEPS) * far

    def sources(block):
        field = [[joule[layer, block * 4 + k] for k in range(4)] for layer in range(LAYERS)]

        def depth(n, carry):
            total = [zero] * 4
            for layer in range(LAYERS):
                w = split[layer, base + n]
                total = [total[k] + w * field[layer][k] for k in range(4)]
            for k in range(4):
                source[n, block * 4 + k] = total[k]
            return carry

        lax.fori_loop(0, THICK, depth, 0, unroll=4)

    loop(WIDE // 4, sources)
    for ref in (one, two):
        for row in range(WIDE):
            ref[0, row] = zero
            ref[THICK + 1, row] = zero

    fields = (source, deep_edge, row_edge, col_edge, turn, lane)
    for sweep, src, dst in ((1, warm, one), (2, one, two), (3, two, one)):

        def step(i, sweep=sweep, src=src, dst=dst):
            n = sweep * far + i

            def put(row, value):
                dst[n + 1, row] = value

            relax(n, src, range(sweep, WIDE - sweep), put, *fields)

        loop(THICK - sweep, step, 5)

    for ref, half in ((out, core), (s_out, 1 - core)):

        def final_step(i, ref=ref, half=half):
            def put(row, value):
                ref[i, row - SWEEPS] = value

            relax(SWEEPS * far + DEEP * half + i, one, range(SWEEPS, SWEEPS + ROWS), put, *fields)

        loop(DEEP, final_step)
    weigh(weights, heat_parts(out, s_out), s_final, HALF * (1 - far))


def heat_parts(own, got):
    far, core = place()
    return ((own, 0, SLAB * far + DEEP * core), (got, 0, SLAB * far + DEEP * (1 - core)))


def own_heat_kernel(weights, out, s_out, final):
    far, _ = place()
    weigh(weights, heat_parts(out, s_out), final, HALF * far)


def update_kernel(final, got, a6, mine, send):
    _, core = place()

    def body(n):
        for half, out in ((core, mine), (1 - core, send)):
            o = OWN * half + n
            for k in range(ROWS):
                heat = final[o, k] + got[o, k]
                out[n, k] = (16.0 * a6[1, o, k]) * inverse(1.0 + thermal_slope * heat)

    loop(OWN, body)


def unpack_kernel(own, got, out):
    _, core = place()

    def body(n):
        for k in range(ROWS):
            out[n, core * 2 + k // 8, pl.ds(k % 8, 8, stride=8), :] = own[n, k]
            out[n, (1 - core) * 2 + k // 8, pl.ds(k % 8, 8, stride=8), :] = got[n, k]

    loop(own.shape[0], body)


def unpack(own, got):
    n = own.shape[0]
    out = jax.ShapeDtypeStruct((n, 4, 64, 128), F32)
    return raw_back(call(unpack_kernel, out, cost=n / 10, raw_out=True)(own, got))


def pack(value):
    n = value.shape[0]
    return call(pack_kernel, [shaped(n, ROWS)] * 2, cost=2, raw_in=True)(raw_view(value))


def to_core(value):
    return lax.ppermute(value, "therm", [(i, i ^ 1) for i in range(4)])


def to_far(value):
    return lax.ppermute(value, "therm", [(i, i ^ 2) for i in range(4)])


def to_core_far(value):
    return lax.ppermute(value, "therm", [(i, i ^ 3) for i in range(4)])


def to_tile(value, cross=0):
    pairs = []
    for t in range(lax.axis_size("tile") - 1):
        for half in range(2):
            low = 4 * t + 2 * half + 1
            high = 4 * (t + 1) + 2 * (half ^ cross)
            pairs += [(low, high), (high, low)]
    return lax.ppermute(value, ("tile", "therm"), pairs)


def add_pairs(a, b):
    high, low = pair_add((a[0], a[1]), (b[0], b[1]))
    return jnp.stack([high, low])


def along_core_and_x(values):
    values = add_pairs(values, to_core(values))
    peers = []
    for bits in (2, 3, 1):
        pairs = [
            (4 * t + h, 4 * (t ^ (bits & 1)) + (h ^ (bits & 2)))
            for t in range(lax.axis_size("tile"))
            for h in range(4)
        ]
        peers.append(lax.ppermute(values, ("tile", "therm"), pairs))
    for peer in peers:
        values = add_pairs(values, peer)
    return values


def along_tile(values, unit):
    peers = [
        lax.ppermute(values, "tile", [(t, t ^ (unit * k)) for t in range(lax.axis_size("tile"))])
        for k in (2, 1, 3)
    ]
    for peer in peers:
        values = add_pairs(values, peer)
    return values


def tied(value, to):
    return lax.optimization_barrier((value, to))[0]


def per_device(
    sink_current,
    metal_category,
    upward_link_flag,
    supply_contact_flag,
    baseline_admittance,
    beginning_warmth,
    cell_diffusivity,
    dissipation_split,
    probe_weighting,
):
    weights, split = probe_weighting, dissipation_split.T
    args = [raw_view(v) for v in (sink_current, metal_category, upward_link_flag, supply_contact_flag)]
    t_own, t_send, *fetched = call(
        first_pack_kernel,
        [shaped(DEEP, ROWS)] * 2 + [jax.ShapeDtypeStruct(v.shape, v.dtype) for v in args] + [shaped(8)],
        cost=2,
        raw_in=True,
        hold=lambda i: i in (0, len(args) + 1),
    )(raw_view(beginning_warmth), *args, baseline_admittance)
    t_got = to_core(t_send)
    a_own, a_send = call(pack_args_kernel, [shaped(4 * OWN, ROWS)] * 2, cost=1)(*fetched)
    a_got = to_core(a_send)
    part = call(heat_kernel, shaped(LAYERS, ROWS), scalars=1, cost=3, room=2)(weights, t_own, t_got)
    a6, s_far, s_core_far, s_tile_far, s_core, s_tile = call(
        merge_kernel,
        [
            shaped(4, HALF, ROWS),
            shaped(HEATED + 2, ROWS),
            shaped(HEATED + 2, RIM),
            shaped(HEATED + 2, RIM),
            shaped(HEATED + 4 * HALF, RIM),
            shaped(HEATED * RIM + HALF * SIDE),
        ],
        cost=1.5,
        room=2,
    )(part, a_own, a_got)
    g_far = to_far(s_far)
    g_tile = to_tile(s_tile)
    g_tile_far = to_tile(s_tile_far, 1)
    g_core_far = to_core_far(s_core_far)
    g_core = to_core(s_core)

    k_own, k_send = pack(tied(cell_diffusivity, s_far))

    field = shaped(HALF + 2, EXT)
    coef = shaped(HALF, EXT)
    v0, v1, v2, diag, row_edge, col_edge, vert, ground, s_basis = call(
        basis_kernel,
        [field, field, field, coef, coef, coef, shaped(HALF + 1, EXT), coef, shaped(2, EXT - 4)],
        scratch=((HEATED, EXT), (HALF, EXT)),
        cost=3,
    )(part, a6, g_far, g_core_far, g_tile_far, g_core, g_tile)
    g_basis = to_far(s_basis)
    k_got = to_core(tied(k_send, s_basis))
    rim = shaped(2, SLAB, SWEEPS)
    k_core, k_tile = call(slab_rim_kernel, [rim, rim], cost=0.4)(t_own, t_got, k_own, k_got)
    g_core, g_rim = to_core(k_core), to_tile(k_tile)
    s_deep = call(slab_deep_kernel, shaped(2, DEEP_ROWS), cost=0.3)(t_own, t_got, k_own, k_got, g_core, g_rim)
    w2, sums = call(moments_kernel, [field, shaped(2)], cost=0.9)(
        tied(v0, k_tile), v1, v2, diag, row_edge, col_edge, vert, g_basis
    )
    thick = shaped(THICK, WIDE)
    inner = call(
        slab_inner_kernel, [shaped(THICK + 2, WIDE), thick, shaped(THICK + 1, WIDE), thick, thick, thick], cost=5.5
    )(tied(t_own, sums), t_got, k_own, k_got)
    values = along_core_and_x(sums)
    values, s_deep, inner = lax.optimization_barrier((values, s_deep, inner))
    values = along_tile(values, 2)
    total = along_tile(values, 8)
    total, g_deep = lax.optimization_barrier((total, to_far(s_deep)))

    power, p_core, p_tile, loss, s_loss = call(
        power_kernel,
        [shaped(HALF, ROWS), shaped(HALF, RIM), shaped(HALF, RIM), shaped(OWN, ROWS), shaped(OWN, ROWS)],
        scratch=((HALF + 2, EXT),),
        cost=1.4,
    )(total, v0, v1, w2, diag, row_edge, col_edge, vert, ground, g_basis)
    p_far = to_far(power)
    q_tile = to_tile(p_tile)
    q_tile_far = to_tile(p_tile, 1)
    q_core_far = to_core_far(p_core)
    q_core = to_core(p_core)
    voltage_loss = unpack(loss, to_core(s_loss))

    warm, _, *edges = call(
        slab_outer_kernel,
        [shaped(THICK + 2, WIDE), thick, shaped(THICK + 1, WIDE), thick, thick, thick],
        cost=4,
        alias={i: i for i in range(6)},
    )(*inner, g_core, g_rim, g_deep)
    out, s_out, s_final = call(
        sweeps_kernel,
        [shaped(DEEP, ROWS), shaped(DEEP, ROWS), shaped(HALF, ROWS)],
        scratch=((LAYERS, WIDE), (THICK, WIDE), (THICK + 2, WIDE), (THICK + 2, WIDE)),
        scalars=2,
        cost=14,
        room=14,
    )(split, weights, power, p_far, q_core, q_core_far, q_tile, q_tile_far, warm, *edges)
    g_final = to_far(s_final)
    final = call(own_heat_kernel, shaped(HALF, ROWS), scalars=1, cost=1.4, room=2)(weights, out, s_out)
    final_warmth = unpack(out, to_core(s_out))
    g_final = tied(g_final, final_warmth)
    mine, s_mine = call(update_kernel, [shaped(OWN, ROWS)] * 2, cost=0.4)(final, g_final, a6)
    updated_admittance = unpack(mine, to_core(s_mine))
    return voltage_loss, final_warmth, updated_admittance


def solution(mesh):
    spread = P("therm", "tile", None)
    return jax.shard_map(
        per_device,
        mesh=mesh,
        in_specs=(spread, spread, spread, spread, P(), spread, spread, P(), P()),
        out_specs=(spread, spread, spread),
        check_vma=False,
    )
```

```python
import functools

import jax
import jax.numpy as jnp
from jax import lax
from jax.experimental import pallas as pl
from jax.experimental.pallas import tpu as pltpu
from jax.sharding import PartitionSpec as P


LAYERS = 12
HALF = LAYERS // 2
OWN = 3
DEPTHS = 64
SLAB = DEPTHS // 2
DEEP = 16
ROWS = 16
RIM = 3
SIDE = 2 * RIM + 2 * (RIM - 1)
EXT = ROWS + 2 * RIM
HEATED = 7
SWEEPS = 4
PARTS = 4
WIDE = ROWS + 2 * SWEEPS
THICK = SLAB + SWEEPS
SCALE = 1.0 / 16.0
TINY = 1e-30

shunt_level = 0.05
pad_conductance = 4.0
via_conductance = 2.0
thermal_slope = 0.2
sink_level = 0.1

F32 = jnp.float32


def place():
    therm = lax.axis_index("therm")
    return therm // 2, therm % 2


def shaped(*dims):
    return jax.ShapeDtypeStruct(dims + (8, 128), F32)


def call(kernel, outs, scratch=(), scalars=0, cost=0, raw_in=False, raw_out=False, room=4, alias={}, hold=lambda i: True):
    def held(out):
        return out if raw_out else pltpu.VMEM(out.shape, out.dtype)

    def run(*args):
        smem = [pl.BlockSpec(memory_space=pltpu.SMEM)] * scalars
        fields = args[scalars:]
        space = pltpu.HBM if raw_in else pltpu.VMEM
        fields = [pltpu.with_memory_space_constraint(v, space) for v in fields]
        own = [(pltpu.VMEM if v.ndim > 1 else pltpu.SMEM)(v.shape, v.dtype) for i, v in enumerate(fields) if hold(i)] if raw_in else []
        own += [pltpu.SemaphoreType.DMA((PARTS + len(fields),))] if raw_in else []
        return pl.pallas_call(
            kernel,
            out_shape=jax.tree.map(held, outs),
            in_specs=smem + [pl.BlockSpec(memory_space=space)] * len(fields),
            input_output_aliases=alias,
            out_specs=jax.tree.map(lambda _: pl.BlockSpec(memory_space=pltpu.VMEM), outs),
            scratch_shapes=[pltpu.VMEM(dims + (8, 128), F32) for dims in scratch] + own,
            compiler_params=pltpu.CompilerParams(vmem_limit_bytes=room * 1024 * 1024),
            cost_estimate=pl.CostEstimate(flops=0, bytes_accessed=int(cost * 3.4e6), transcendentals=0),
        )(*args[:scalars], *fields)

    return run


def raw_view(value):
    n, rows, width = value.shape
    split = value.reshape(n, rows // 8, 8, width // 128, 128).transpose(0, 1, 3, 2, 4)
    return split.reshape(n, rows // 8, 8 * (width // 128), 128)


def raw_back(value):
    n, blocks, high, lanes = value.shape
    split = value.reshape(n, blocks, high // 8, 8, lanes).transpose(0, 1, 3, 2, 4)
    return split.reshape(n, blocks * 8, (high // 8) * lanes)


def at_row(ref, n, chunk, row):
    return ref[n, chunk * 2 + row // 8, pl.ds(row % 8, 8, stride=8), :]


def loop(count, body, unroll=8):
    def step(i, carry):
        body(i)
        return carry

    lax.fori_loop(0, count, step, 0, unroll=min(unroll, count))


def iotas():
    return lax.broadcasted_iota(jnp.int32, (8, 128), 0), lax.broadcasted_iota(jnp.int32, (8, 128), 1)


def after(v, lane):
    r = pltpu.roll(v, 127, 1)
    return jnp.where(lane == 127, pltpu.roll(r, 7, 0), r)


def before(v, lane):
    r = pltpu.roll(v, 1, 1)
    return jnp.where(lane == 0, pltpu.roll(r, 1, 0), r)


def inverse(v):
    r = pl.reciprocal(v, approx=True)
    r = r * (2.0 - v * r)
    return r * (2.0 - v * r)


def harmonic(a, b):
    return a * b * inverse(jnp.maximum(a + b, TINY))


def pack_field(value, held, sems):
    size = value.shape[0] // PARTS
    copies = [
        pltpu.make_async_copy(value.at[pl.ds(p * size, size)], held.at[pl.ds(p * size, size)], sems.at[p])
        for p in range(PARTS)
    ]
    for copy in copies:
        copy.start()

    def finish(own, send):
        _, core = place()
        for p, copy in enumerate(copies):
            copy.wait()

            def body(i, p=p):
                n = p * size + i
                for row in range(ROWS):
                    own[n, row] = at_row(held, n, core, row)
                    send[n, row] = at_row(held, n, 1 - core, row)

            loop(size, body)

    return finish


def pack_kernel(value, own, send, held, sems):
    pack_field(value, held, sems)(own, send)


def first_pack_kernel(
    value, sink, category, link, contact, classes, t_own, t_send, sink_, category_, link_, contact_, table, held, classes_, sems
):
    finish = pack_field(value, held, sems)
    raw = ((classes, classes_), (sink, sink_), (category, category_), (link, link_), (contact, contact_))
    copies = [pltpu.make_async_copy(ref, to, sems.at[PARTS + p]) for p, (ref, to) in enumerate(raw)]
    for copy in copies:
        copy.start()
    finish(t_own, t_send)
    for copy in copies:
        copy.wait()
    for number in range(8):
        table[number] = jnp.full((8, 128), classes_[number] * SCALE, F32)


def pack_args_kernel(sink, category, link, contact, classes, own, send):
    _, core = place()

    def body(n):
        for row in range(ROWS):
            for chunk, out in ((core, own), (1 - core, send)):
                kind = at_row(category, n, chunk, row)
                table = classes[0]
                for number in range(1, 8):
                    table = jnp.where(kind == number, classes[number], table)
                out[n, row] = at_row(sink, n, chunk, row)
                out[OWN + n, row] = table
                out[2 * OWN + n, row] = at_row(link, n, chunk, row).astype(F32) * (via_conductance * SCALE)
                out[3 * OWN + n, row] = at_row(contact, n, chunk, row).astype(F32) * (
                    pad_conductance * SCALE
                ) + (shunt_level * SCALE)

    loop(OWN, body)


def weigh(weights, parts, acc, first_layer=0):
    layers, rows = acc.shape[:2]
    size = 48 // layers

    def block_of(block):
        total = [jnp.zeros((8, 128), F32)] * (size * layers)
        for ref, first, base in parts:

            def step(z, total):
                field = [ref[first + z, block * size + k] for k in range(size)]
                out = []
                for layer in range(layers):
                    w = weights[first_layer + layer, base + z]
                    out += [total[layer * size + k] + w * field[k] for k in range(size)]
                return tuple(out)

            total = lax.fori_loop(0, DEEP, step, tuple(total), unroll=16)
        for layer in range(layers):
            for k in range(size):
                acc[layer, block * size + k] = total[layer * size + k]

    loop(rows // size, block_of, 1)


def heat_kernel(weights, t_own, t_got, part):
    weigh(weights, heat_parts(t_own, t_got), part)


def merge_kernel(part, a_own, a_got, a6, s_far, s_core_far, s_tile_far, s_core, s_tile):
    far, core = place()

    def merge(n):
        for row in range(ROWS):
            for ch in range(4):
                a6[ch, OWN * core + n, row] = a_own[ch * OWN + n, row]
                a6[ch, OWN * (1 - core) + n, row] = a_got[ch * OWN + n, row]

    loop(OWN, merge)
    to_core, to_tile = (ROWS - RIM) * (1 - core), (ROWS - RIM) * core

    def heats(n):
        for row in range(ROWS):
            s_far[n, row] = part[5 * (1 - far) + n, row]
        for k in range(RIM):
            s_core_far[n, k] = part[5 * (1 - far) + n, to_core + k]
            s_tile_far[n, k] = part[5 * (1 - far) + n, to_tile + k]
            s_core[n, k] = part[5 * far + n, to_core + k]
            s_tile[n * RIM + k] = part[5 * far + n, to_tile + k]

    loop(HEATED, heats)
    edge = 5 * (1 - far)
    for n, ch in ((HEATED, 0), (HEATED + 1, 2)):
        for row in range(ROWS):
            s_far[n, row] = a6[ch, edge, row]
        for k in range(RIM):
            s_core_far[n, k] = a6[ch, edge, to_core + k]
            s_tile_far[n, k] = a6[ch, edge, to_tile + k]

    def args(o):
        for ch in range(4):
            for k in range(RIM):
                s_core[HEATED + ch * HALF + o, k] = a6[ch, o, to_core + k]
        first = HEATED * RIM + o * SIDE
        for k in range(RIM):
            s_tile[first + k] = a6[0, o, to_tile + k]
            s_tile[first + RIM + k] = a6[1, o, to_tile + k]
        for k in range(RIM - 1):
            s_tile[first + 2 * RIM + k] = a6[2, o, to_tile + core + k]
            s_tile[first + 3 * RIM - 1 + k] = a6[3, o, to_tile + core + k]

    loop(HALF, args)


def apply(v, o, row, diag, row_edge, col_edge, vert, lane):
    here = v[o + 1, row]
    ce = col_edge[o, row]
    return (
        diag[o, row] * here
        - row_edge[o, row - 1] * v[o + 1, row - 1]
        - row_edge[o, row] * v[o + 1, row + 1]
        - ce * after(here, lane)
        - before(ce * here, lane)
        - vert[o + 1, row] * v[o + 2, row]
        - vert[o, row] * v[o, row]
    )


def basis_kernel(
    part, a6, g_far, g_core_far, g_tile_far, g_core, g_tile,
    v0, v1, v2, diag, row_edge, col_edge, vert, ground, s_basis, inv, lat,
):
    far, core = place()
    sub, lane = iotas()
    from_core, from_tile = (EXT - RIM) * (1 - core), (EXT - RIM) * core
    zero = jnp.zeros((8, 128), F32)

    def heats(n):
        def one(row, heat):
            inv[n, row] = inverse(1.0 + thermal_slope * heat)

        for k in range(ROWS):
            one(RIM + k, part[5 * far + n, k] + g_far[n, k])
        for k in range(RIM):
            one(from_core + k, g_core[n, k] + g_core_far[n, k])
            one(from_tile + k, g_tile[n * RIM + k] + g_tile_far[n, k])

    loop(HEATED, heats)
    lower = far.astype(F32)
    halo, none = 7 * (1 - far), 7 * far

    def rim(row, b, up):
        v0[halo, row] = b
        v0[none, row] = zero
        vert[0, row] = up * inv[0, row] * lower

    for k in range(ROWS):
        rim(RIM + k, g_far[HEATED, k], g_far[HEATED + 1, k])
    for k in range(RIM):
        rim(from_core + k, g_core_far[HEATED, k], g_core_far[HEATED + 1, k])
        rim(from_tile + k, g_tile_far[HEATED, k], g_tile_far[HEATED + 1, k])
    for row in range(EXT):
        for edge in (0, 7):
            v1[edge, row] = zero
            v2[edge, row] = zero

    def fields(o):
        def one(row, b, g, up, gr):
            warm = inv[o + far, row]
            v0[o + 1, row] = b
            lat[o, row] = g * warm
            vert[o + 1, row] = up * warm
            ground[o, row] = gr

        for k in range(ROWS):
            one(RIM + k, *[a6[ch, o, k] for ch in range(4)])
        for k in range(RIM):
            one(from_core + k, *[g_core[HEATED + ch * HALF + o, k] for ch in range(4)])
        first = HEATED * RIM + o * SIDE
        for k in range(RIM):
            v0[o + 1, from_tile + k] = g_tile[first + k]
            lat[o, from_tile + k] = g_tile[first + RIM + k] * inv[o + far, from_tile + k]
        for k in range(RIM - 1):
            row = from_tile + 1 - core + k
            vert[o + 1, row] = g_tile[first + 2 * RIM + k] * inv[o + far, row]
            ground[o, row] = g_tile[first + 3 * RIM - 1 + k]

    loop(HALF, fields)
    last = (sub == 7) & (lane == 127)

    def edges(o):
        for row in range(EXT - 1):
            row_edge[o, row] = harmonic(lat[o, row], lat[o, row + 1])
        for row in range(1, EXT - 1):
            here = lat[o, row]
            ce = jnp.where(last, 0.0, harmonic(here, after(here, lane)))
            col_edge[o, row] = ce
            diag[o, row] = (
                ground[o, row] + vert[o + 1, row] + vert[o, row]
                + row_edge[o, row - 1] + row_edge[o, row] + ce + before(ce, lane)
            )

    loop(HALF, edges)

    def first(o):
        for row in range(1, EXT - 1):
            v1[o + 1, row] = apply(v0, o, row, diag, row_edge, col_edge, vert, lane)

    loop(HALF, first)

    def second(o):
        for row in range(2, EXT - 2):
            v2[o + 1, row] = apply(v1, o, row, diag, row_edge, col_edge, vert, lane)

    loop(HALF, second)
    edge = 5 * (1 - far) + 1
    for k in range(EXT - 4):
        s_basis[0, k] = v1[edge, 2 + k]
        s_basis[1, k] = v2[edge, 2 + k]


def moments_kernel(v0, v1, v2, diag, row_edge, col_edge, vert, got, w2, out):
    far, _ = place()
    _, lane = iotas()

    def copy(n):
        for row in range(2, EXT - 2):
            w2[n, row] = v2[n, row]

    loop(HALF + 2, copy)
    edge, halo = 5 * (1 - far) + 1, 7 * (1 - far)
    for k in range(EXT - 4):
        row = 2 + k
        link = vert[6 * (1 - far), row]
        w2[edge, row] = v2[edge, row] - link * got[0, k]
        w2[halo, row] = got[1, k] - link * v1[edge, row]

    def body(o, sums):
        sums = list(sums)
        for row in range(RIM, RIM + ROWS):
            a, b, c = v0[o + 1, row], v1[o + 1, row], w2[o + 1, row]
            d = apply(w2, o, row, diag, row_edge, col_edge, vert, lane)
            for n, term in enumerate((a * a, a * b, b * b, b * c, c * c, c * d)):
                sums[n] = sums[n] + term
        return tuple(sums)

    sums = lax.fori_loop(0, HALF, body, (jnp.zeros((8, 128), F32),) * 6)
    for n in range(6):
        out[0, pl.ds(n, 1), :] = jnp.full((1, 128), jnp.sum(sums[n]), F32)
    out[0, pl.ds(6, 2), :] = jnp.zeros((2, 128), F32)
    out[1] = jnp.zeros((8, 128), F32)


def two_sum(a, b):
    s = a + b
    t = s - a
    return s, (a - (s - t)) + (b - t)


def two_prod(a, b):
    def split(v):
        t = v * 4097.0
        high = t - (t - v)
        return high, v - high

    p = a * b
    (ah, al), (bh, bl) = split(a), split(b)
    return p, ((ah * bh - p) + ah * bl + al * bh) + al * bl


def pair_add(a, b):
    s, e = two_sum(a[0], b[0])
    e = e + (a[1] + b[1])
    high = s + e
    return high, e - (high - s)


def pair_mul(a, b):
    p, e = two_prod(a[0], b[0])
    e = e + (a[0] * b[1] + a[1] * b[0])
    high = p + e
    return high, e - (high - p)


def pair_neg(a):
    return -a[0], -a[1]


def pair_div(a, b):
    q = a[0] / b[0]
    r = pair_add(a, pair_neg(pair_mul(b, (q, jnp.zeros_like(q)))))
    q2 = (r[0] + r[1]) / b[0]
    high = q + q2
    return high, q2 - (high - q)


def coefficients(m):
    mean, m2, m3, m4, m5 = [pair_div(v, m[0]) for v in m[1:]]
    low = pair_neg(mean)

    def lowered(seq):
        return [pair_add(b, pair_mul(low, a)) for a, b in zip(seq, seq[1:])]

    one = (jnp.ones_like(mean[0]), jnp.zeros_like(mean[0]))
    seq = [one, mean, m2, m3, m4, m5]
    seq = lowered(seq)
    central = []
    for power in range(2, 6):
        seq = lowered(seq)
        central.append(seq[0])
    c2, c3, c4, c5 = [v[0] + v[1] for v in central]
    s = mean[0] + mean[1]
    ok1 = c2 > 3e-8 * s * s
    c2 = jnp.where(ok1, c2, 1.0)
    skew = c3 / c2
    n2 = c4 - skew * c3 - c2 * c2
    ok2 = ok1 & (n2 > 1e-6 * c2 * c2) & (n2 > 3e-8 * (s * s) * (s * s))
    n2 = jnp.where(ok2, n2, 1.0)
    tq = c5 - 2.0 * skew * c4 + (skew * skew - 2.0 * c2) * c3 + 2.0 * skew * c2 * c2
    a2 = s + tq / n2
    a1 = s + skew
    b1, b2 = c2, n2 / c2
    d0 = s
    d1 = a1 - b1 / d0
    d2 = a2 - b2 / d1
    y0 = 1.0 / d0
    y1 = jnp.where(ok1, -y0 / d1, 0.0)
    y2 = jnp.where(ok2, -y1 / d2, 0.0)
    z2 = y2
    z1 = y1 - jnp.where(ok2, b2 * z2 / d1, 0.0)
    z0 = y0 - jnp.where(ok1, b1 * z1 / d0, 0.0)
    k2 = z2
    k1 = z1 - z2 * (skew + 2.0 * s)
    k0 = z0 - z1 * s + z2 * (s * s + skew * s - c2)
    return k0 * SCALE, k1 * SCALE, k2 * SCALE


def power_kernel(
    total, v0, v1, w2, diag, row_edge, col_edge, vert, ground, got,
    power, s_core, s_tile, loss, s_loss, volts,
):
    far, core = place()
    _, lane = iotas()
    spread = [
        (
            jnp.broadcast_to(total[0, pl.ds(n, 1), :], (8, 128)),
            jnp.broadcast_to(total[1, pl.ds(n, 1), :], (8, 128)),
        )
        for n in range(6)
    ]
    c0, c1, c2 = coefficients(spread)
    halo = 7 * (1 - far)

    def combine(n):
        for row in range(2, EXT - 2):
            volts[n, row] = c0 * v0[n, row] + c1 * v1[n, row] + c2 * w2[n, row]

    loop(HALF + 2, combine)
    for k in range(EXT - 4):
        row = 2 + k
        volts[halo, row] = c0 * v0[halo, row] + c1 * got[0, k] + c2 * w2[halo, row]

    def body(o):
        for k in range(ROWS):
            row = RIM + k
            x = volts[o + 1, row]
            near = after(x, lane) - x
            q = col_edge[o, row] * near * near
            q = q + before(q, lane)
            for edge, other in (
                (row_edge[o, row - 1], volts[o + 1, row - 1]),
                (row_edge[o, row], volts[o + 1, row + 1]),
                (vert[o + 1, row], volts[o + 2, row]),
                (vert[o, row], volts[o, row]),
            ):
                d = x - other
                q = q + edge * d * d
            power[o, k] = 16.0 * ground[o, row] * x * x + 8.0 * q

    loop(HALF, body)
    to_core, to_tile = (ROWS - RIM) * (1 - core), (ROWS - RIM) * core

    def sides(o):
        for k in range(RIM):
            s_core[o, k] = power[o, to_core + k]
            s_tile[o, k] = power[o, to_tile + k]

    loop(HALF, sides)

    def outs(n):
        for k in range(ROWS):
            loss[n, k] = volts[1 + OWN * core + n, RIM + k]
            s_loss[n, k] = volts[1 + OWN * (1 - core) + n, RIM + k]

    loop(OWN, outs)


def slab_rim_kernel(t_own, t_got, k_own, k_got, s_core, s_tile):
    _, core = place()
    to_core, to_tile = (ROWS - SWEEPS) * (1 - core), (ROWS - SWEEPS) * core

    def body(n):
        for f, (own, got) in enumerate(((t_own, t_got), (k_own, k_got))):
            for ref, z in ((own, DEEP * core + n), (got, DEEP * (1 - core) + n)):
                for k in range(SWEEPS):
                    s_core[f, z, k] = ref[n, to_core + k]
                    s_tile[f, z, k] = ref[n, to_tile + k]

    loop(DEEP, body)


def deep_rows(step):
    return range(step, WIDE - step), sum(WIDE - 2 * k for k in range(1, step))


DEEP_ROWS = deep_rows(SWEEPS + 1)[1]


def slab_deep_kernel(t_own, t_got, k_own, k_got, g_core, g_tile, s_far):
    far, core = place()

    def side(half, number):
        fields = (t_own, k_own) if number == 1 - half else (t_got, k_got)
        top, bottom = (g_core, g_tile) if number else (g_tile, g_core)
        for step in range(1, SWEEPS + 1):
            rows, start = deep_rows(step)
            n = step - 1 if half else DEEP - step
            z = step - 1 if half else SLAB - step
            for i, row in enumerate(rows):
                for f in range(2):
                    if row < SWEEPS:
                        s_far[f, start + i] = top[f, z, row]
                    elif row < SWEEPS + ROWS:
                        s_far[f, start + i] = fields[f][n, row - SWEEPS]
                    else:
                        s_far[f, start + i] = bottom[f, z, row - SWEEPS - ROWS]

    for half in range(2):
        for number in range(2):
            pl.when((far == half) & (core == number))(functools.partial(side, half, number))


def row_edges_of(n, rows, cond, row_edge):
    for row in rows:
        row_edge[n, row] = harmonic(cond[n, row], cond[n, row + 1])


def col_edges_of(n, rows, cond, col_edge):
    sub, lane = iotas()
    last = (sub == 7) & (lane == 127)
    for row in rows:
        here = cond[n, row]
        col_edge[n, row] = jnp.where(last, 0.0, harmonic(here, after(here, lane)))


def deep_edges_of(n, rows, cond, deep_edge):
    for row in rows:
        deep_edge[n + 1, row] = harmonic(cond[n, row], cond[n + 1, row])


def turns_of(n, rows, deep_edge, row_edge, col_edge, turn):
    _, lane = iotas()
    for row in rows:
        ce = col_edge[n, row]
        turn[n, row] = inverse(
            sink_level + deep_edge[n, row] + deep_edge[n + 1, row]
            + row_edge[n, row - 1] + row_edge[n, row] + ce + before(ce, lane)
        )


OUTER = (*range(1, SWEEPS), *range(SWEEPS + ROWS, WIDE - 1))


def slab_inner_kernel(t_own, t_got, k_own, k_got, warm, cond, deep_edge, row_edge, col_edge, turn):
    far, core = place()
    zero = jnp.zeros((8, 128), F32)
    base = SWEEPS * far

    def body(n):
        for own, got, out, up in ((t_own, t_got, warm, 1), (k_own, k_got, cond, 0)):
            for ref, z in ((own, DEEP * core + n), (got, DEEP * (1 - core) + n)):
                for k in range(ROWS):
                    out[up + base + z, SWEEPS + k] = ref[n, k]

    loop(DEEP, body)
    for row in range(WIDE):
        for n in (0, THICK + 1):
            warm[n, row] = zero
        for n in (0, THICK):
            deep_edge[n, row] = zero
    mid = range(SWEEPS, SWEEPS + ROWS)

    def between(z):
        deep_edges_of(base + z, mid, cond, deep_edge)

    loop(SLAB - 1, between)

    def level(z):
        row_edges_of(base + z, mid[:-1], cond, row_edge)
        col_edges_of(base + z, mid, cond, col_edge)

    loop(SLAB, level)

    def turns(z):
        turns_of(base + 1 + z, mid[1:-1], deep_edge, row_edge, col_edge, turn)

    loop(SLAB - 2, turns)


def slab_outer_kernel(
    warm_in, cond_in, deep_in, row_in, col_in, turn_in, g_core, g_tile, g_far,
    warm, cond, deep_edge, row_edge, col_edge, turn,
):
    far, core = place()
    zero = jnp.zeros((8, 128), F32)
    base = SWEEPS * far
    from_core, from_tile = (WIDE - SWEEPS) * (1 - core), (WIDE - SWEEPS) * core

    def body(z):
        for f, out, up in ((0, warm, 1), (1, cond, 0)):
            for k in range(SWEEPS):
                out[up + base + z, from_core + k] = g_core[f, z, k]
                out[up + base + z, from_tile + k] = g_tile[f, z, k]

    loop(SLAB, body)
    for step in range(1, SWEEPS + 1):
        at = jnp.where(far == 0, SLAB + step - 1, SWEEPS - step)
        rows, start = deep_rows(step)
        for f, out, up in ((0, warm, 1), (1, cond, 0)):
            for row in range(WIDE):
                out[up + at, row] = g_far[f, start + row - step] if row in rows else zero
    every = range(1, WIDE - 1)

    def between(n):
        deep_edges_of(n, OUTER, cond, deep_edge)

    loop(THICK - 1, between)

    def meeting(i):
        deep_edges_of((SLAB - 1) * (1 - far) + i, range(SWEEPS, SWEEPS + ROWS), cond, deep_edge)

    loop(SWEEPS, meeting)

    def level(z):
        row_edges_of(base + z, (*range(SWEEPS), *range(SWEEPS + ROWS - 1, WIDE - 1)), cond, row_edge)
        col_edges_of(base + z, OUTER, cond, col_edge)

    loop(SLAB, level)

    def halo_level(i):
        n = SLAB * (1 - far) + i
        row_edges_of(n, range(WIDE - 1), cond, row_edge)
        col_edges_of(n, every, cond, col_edge)

    loop(SWEEPS, halo_level)

    def turns(z):
        rows = (*range(1, SWEEPS + 1), *range(SWEEPS + ROWS - 1, WIDE - 1))
        turns_of(base + z, rows, deep_edge, row_edge, col_edge, turn)

    loop(SLAB, turns)

    def more_turns(i):
        turns_of((SLAB - 1) * (1 - far) + far + i, every, deep_edge, row_edge, col_edge, turn)

    loop(SWEEPS, more_turns)
    turns_of(0, every, deep_edge, row_edge, col_edge, turn)
    turns_of(THICK - 1, every, deep_edge, row_edge, col_edge, turn)


def relax(n, src, rows, put, source, deep_edge, row_edge, col_edge, turn, lane):
    above, here, e_above = src[n + 1, rows[0] - 1], src[n + 1, rows[0]], row_edge[n, rows[0] - 1]
    for row in rows:
        under, e_under, ce = src[n + 1, row + 1], row_edge[n, row], col_edge[n, row]
        flow = source[n, row] + ce * after(here, lane) + before(ce * here, lane)
        flow = flow + e_above * above + e_under * under
        flow = flow + deep_edge[n, row] * src[n, row] + deep_edge[n + 1, row] * src[n + 2, row]
        put(row, flow * turn[n, row])
        above, here, e_above = here, under, e_under


def sweeps_kernel(
    split, weights, power, p_far, p_core, p_core_far, p_tile, p_tile_far,
    warm, deep_edge, row_edge, col_edge, turn,
    out, s_out, s_final,
    joule, source, one, two,
):
    far, core = place()
    _, lane = iotas()
    zero = jnp.zeros((8, 128), F32)
    from_core = 1 + (EXT - RIM) * (1 - core)
    from_tile = 1 + (EXT - RIM) * core

    def gather(o):
        for layer, mid, by_core, by_tile in (
            (HALF * far + o, power, p_core, p_tile),
            (HALF * (1 - far) + o, p_far, p_core_far, p_tile_far),
        ):
            for k in range(ROWS):
                joule[layer, SWEEPS + k] = mid[o, k]
            for k in range(RIM):
                joule[layer, from_core + k] = by_core[o, k]
                joule[layer, from_tile + k] = by_tile[o, k]
            joule[layer, 0] = zero
            joule[layer, WIDE - 1] = zero

    loop(HALF, gather)
    base = (SLAB - SWEEPS) * far

    def sources(block):
        field = [[joule[layer, block * 4 + k] for k in range(4)] for layer in range(LAYERS)]

        def depth(n, carry):
            total = [zero] * 4
            for layer in range(LAYERS):
                w = split[layer, base + n]
                total = [total[k] + w * field[layer][k] for k in range(4)]
            for k in range(4):
                source[n, block * 4 + k] = total[k]
            return carry

        lax.fori_loop(0, THICK, depth, 0, unroll=9)

    loop(WIDE // 4, sources)
    for ref in (one, two):
        for row in range(WIDE):
            ref[0, row] = zero
            ref[THICK + 1, row] = zero

    fields = (source, deep_edge, row_edge, col_edge, turn, lane)
    for sweep, src, dst in ((1, warm, one), (2, one, two), (3, two, one)):

        def step(i, sweep=sweep, src=src, dst=dst):
            n = sweep * far + i

            def put(row, value):
                dst[n + 1, row] = value

            relax(n, src, range(sweep, WIDE - sweep), put, *fields)

        loop(THICK - sweep, step, 7)

    for ref, half in ((out, core), (s_out, 1 - core)):

        def final_step(i, ref=ref, half=half):
            def put(row, value):
                ref[i, row - SWEEPS] = value

            relax(SWEEPS * far + DEEP * half + i, one, range(SWEEPS, SWEEPS + ROWS), put, *fields)

        loop(DEEP, final_step, 8)
    weigh(weights, heat_parts(out, s_out), s_final, HALF * (1 - far))


def heat_parts(own, got):
    far, core = place()
    return ((own, 0, SLAB * far + DEEP * core), (got, 0, SLAB * far + DEEP * (1 - core)))


def own_heat_kernel(weights, out, s_out, final):
    far, _ = place()
    weigh(weights, heat_parts(out, s_out), final, HALF * far)


def update_kernel(final, got, a6, mine, send):
    _, core = place()

    def body(n):
        for half, out in ((core, mine), (1 - core, send)):
            o = OWN * half + n
            for k in range(ROWS):
                heat = final[o, k] + got[o, k]
                out[n, k] = (16.0 * a6[1, o, k]) * inverse(1.0 + thermal_slope * heat)

    loop(OWN, body)


def unpack_kernel(own, got, out):
    _, core = place()

    def body(n):
        for k in range(ROWS):
            out[n, core * 2 + k // 8, pl.ds(k % 8, 8, stride=8), :] = own[n, k]
            out[n, (1 - core) * 2 + k // 8, pl.ds(k % 8, 8, stride=8), :] = got[n, k]

    loop(own.shape[0], body)


def unpack(own, got):
    n = own.shape[0]
    out = jax.ShapeDtypeStruct((n, 4, 64, 128), F32)
    return raw_back(call(unpack_kernel, out, cost=n / 10, raw_out=True)(own, got))


def pack(value):
    n = value.shape[0]
    return call(pack_kernel, [shaped(n, ROWS)] * 2, cost=2, raw_in=True)(raw_view(value))


def to_core(value):
    return lax.ppermute(value, "therm", [(i, i ^ 1) for i in range(4)])


def to_far(value):
    return lax.ppermute(value, "therm", [(i, i ^ 2) for i in range(4)])


def to_core_far(value):
    return lax.ppermute(value, "therm", [(i, i ^ 3) for i in range(4)])


def to_tile(value, cross=0):
    pairs = []
    for t in range(lax.axis_size("tile") - 1):
        for half in range(2):
            low = 4 * t + 2 * half + 1
            high = 4 * (t + 1) + 2 * (half ^ cross)
            pairs += [(low, high), (high, low)]
    return lax.ppermute(value, ("tile", "therm"), pairs)


def add_pairs(a, b):
    high, low = pair_add((a[0], a[1]), (b[0], b[1]))
    return jnp.stack([high, low])


def along_core_and_x(values):
    values = add_pairs(values, to_core(values))
    peers = []
    for bits in (2, 3, 1):
        pairs = [
            (4 * t + h, 4 * (t ^ (bits & 1)) + (h ^ (bits & 2)))
            for t in range(lax.axis_size("tile"))
            for h in range(4)
        ]
        peers.append(lax.ppermute(values, ("tile", "therm"), pairs))
    for peer in peers:
        values = add_pairs(values, peer)
    return values


def along_tile(values, unit):
    peers = [
        lax.ppermute(values, "tile", [(t, t ^ (unit * k)) for t in range(lax.axis_size("tile"))])
        for k in (2, 1, 3)
    ]
    for peer in peers:
        values = add_pairs(values, peer)
    return values


def tied(value, to):
    return lax.optimization_barrier((value, to))[0]


def per_device(
    sink_current,
    metal_category,
    upward_link_flag,
    supply_contact_flag,
    baseline_admittance,
    beginning_warmth,
    cell_diffusivity,
    dissipation_split,
    probe_weighting,
):
    weights, split = probe_weighting, dissipation_split.T
    args = [raw_view(v) for v in (sink_current, metal_category, upward_link_flag, supply_contact_flag)]
    t_own, t_send, *fetched = call(
        first_pack_kernel,
        [shaped(DEEP, ROWS)] * 2 + [jax.ShapeDtypeStruct(v.shape, v.dtype) for v in args] + [shaped(8)],
        cost=2,
        raw_in=True,
        hold=lambda i: i in (0, len(args) + 1),
    )(raw_view(beginning_warmth), *args, baseline_admittance)
    t_got = to_core(t_send)
    a_own, a_send = call(pack_args_kernel, [shaped(4 * OWN, ROWS)] * 2, cost=1)(*fetched)
    a_got = to_core(a_send)
    part = call(heat_kernel, shaped(LAYERS, ROWS), scalars=1, cost=3, room=2)(weights, t_own, t_got)
    a6, s_far, s_core_far, s_tile_far, s_core, s_tile = call(
        merge_kernel,
        [
            shaped(4, HALF, ROWS),
            shaped(HEATED + 2, ROWS),
            shaped(HEATED + 2, RIM),
            shaped(HEATED + 2, RIM),
            shaped(HEATED + 4 * HALF, RIM),
            shaped(HEATED * RIM + HALF * SIDE),
        ],
        cost=1.5,
        room=2,
    )(part, a_own, a_got)
    g_far = to_far(s_far)
    g_tile = to_tile(s_tile)
    g_tile_far = to_tile(s_tile_far, 1)
    g_core_far = to_core_far(s_core_far)
    g_core = to_core(s_core)

    k_own, k_send = pack(tied(cell_diffusivity, s_far))

    field = shaped(HALF + 2, EXT)
    coef = shaped(HALF, EXT)
    v0, v1, v2, diag, row_edge, col_edge, vert, ground, s_basis = call(
        basis_kernel,
        [field, field, field, coef, coef, coef, shaped(HALF + 1, EXT), coef, shaped(2, EXT - 4)],
        scratch=((HEATED, EXT), (HALF, EXT)),
        cost=3,
    )(part, a6, g_far, g_core_far, g_tile_far, g_core, g_tile)
    g_basis = to_far(s_basis)
    k_got = to_core(tied(k_send, s_basis))
    rim = shaped(2, SLAB, SWEEPS)
    k_core, k_tile = call(slab_rim_kernel, [rim, rim], cost=0.4)(t_own, t_got, k_own, k_got)
    g_core, g_rim = to_core(k_core), to_tile(k_tile)
    s_deep = call(slab_deep_kernel, shaped(2, DEEP_ROWS), cost=0.3)(t_own, t_got, k_own, k_got, g_core, g_rim)
    w2, sums = call(moments_kernel, [field, shaped(2)], cost=0.9)(
        tied(v0, k_tile), v1, v2, diag, row_edge, col_edge, vert, g_basis
    )
    thick = shaped(THICK, WIDE)
    inner = call(
        slab_inner_kernel, [shaped(THICK + 2, WIDE), thick, shaped(THICK + 1, WIDE), thick, thick, thick], cost=5.5
    )(tied(t_own, sums), t_got, k_own, k_got)
    values = along_core_and_x(sums)
    values, s_deep, inner = lax.optimization_barrier((values, s_deep, inner))
    values = along_tile(values, 2)
    total = along_tile(values, 8)
    total, g_deep = lax.optimization_barrier((total, to_far(s_deep)))

    power, p_core, p_tile, loss, s_loss = call(
        power_kernel,
        [shaped(HALF, ROWS), shaped(HALF, RIM), shaped(HALF, RIM), shaped(OWN, ROWS), shaped(OWN, ROWS)],
        scratch=((HALF + 2, EXT),),
        cost=1.4,
    )(total, v0, v1, w2, diag, row_edge, col_edge, vert, ground, g_basis)
    p_far = to_far(power)
    q_tile = to_tile(p_tile)
    q_tile_far = to_tile(p_tile, 1)
    q_core_far = to_core_far(p_core)
    q_core = to_core(p_core)
    voltage_loss = unpack(loss, to_core(s_loss))

    warm, _, *edges = call(
        slab_outer_kernel,
        [shaped(THICK + 2, WIDE), thick, shaped(THICK + 1, WIDE), thick, thick, thick],
        cost=4,
        alias={i: i for i in range(6)},
    )(*inner, g_core, g_rim, g_deep)
    out, s_out, s_final = call(
        sweeps_kernel,
        [shaped(DEEP, ROWS), shaped(DEEP, ROWS), shaped(HALF, ROWS)],
        scratch=((LAYERS, WIDE), (THICK, WIDE), (THICK + 2, WIDE), (THICK + 2, WIDE)),
        scalars=2,
        cost=14,
        room=14,
    )(split, weights, power, p_far, q_core, q_core_far, q_tile, q_tile_far, warm, *edges)
    g_final = to_far(s_final)
    final = call(own_heat_kernel, shaped(HALF, ROWS), scalars=1, cost=1.4, room=2)(weights, out, s_out)
    final_warmth = unpack(out, to_core(s_out))
    g_final = tied(g_final, final_warmth)
    mine, s_mine = call(update_kernel, [shaped(OWN, ROWS)] * 2, cost=0.4)(final, g_final, a6)
    updated_admittance = unpack(mine, to_core(s_mine))
    return voltage_loss, final_warmth, updated_admittance


def solution(mesh):
    spread = P("therm", "tile", None)
    return jax.shard_map(
        per_device,
        mesh=mesh,
        in_specs=(spread, spread, spread, spread, P(), spread, spread, P(), P()),
        out_specs=(spread, spread, spread),
        check_vma=False,
    )
```
